256 devices in a mesh: tensor: 64 (over y, z, core), contract: 4 (over x).
Axes of the slice: x: 4, y: 4, z: 8, core: 2. Of those that a mesh axis runs over, the one named last changes fastest.
Arguments:
- amplitudes: float32 [256, 128, 128], P('tensor', 'contract'), may hold values from -6 to 6
- ladder_ints: float32 [128, 128, 16384], P('contract', None, 'tensor'), may hold values from -0.046875 to 0.046875
- cycle_ints: float32 [16, 128, 16, 128], P(None, None, None, 'contract'), may hold values from -0.125 to 0.125
- occ_energy: float32 [16], replicated, may hold values from -2 to -0.5
- virt_energy: float32 [128], replicated, may hold values from 0.5 to 3
Outputs:
- update: float32 [256, 128, 128], P(('tensor', 'contract'))
The draws below stay inside these ranges and needn't reach their ends.
All inputs are finite; a program needn't handle non-finite values.
Results may differ from the reference program's by a relative error of at most 0.00007.
Values sent between devices are 32-bit elements; how exact they have to be, the bound alone decides.
A program may use at most 64 MiB of HBM per device.

```python
import jax
import jax.numpy as jnp
from jax import lax

NOCC = 16
VA = 128
PAIRS = 256


def shard_levels(own_key, shape, split, smallest, top_value):
    loudness, own = 1.0, jax.random.fold_in(own_key, 6)
    for dim, shards_of in split:
        draws = jnp.exp(jax.random.uniform(jax.random.fold_in(own, dim), (shards_of,), jnp.float32, smallest / len(split), top_value / len(split)))
        loudness = loudness * jnp.repeat(draws, shape[dim] // shards_of).reshape([-1 if axis == dim else 1 for axis in range(len(shape))])
    return loudness


def bell_draw(rng, shape, width, most, cuts=(), dtype=jnp.bfloat16):
    values = jax.random.normal(rng, shape, jnp.float32) * width
    if len(cuts) > 0:
        values = shard_levels(rng, shape, cuts, -0.22, 0.18) * values
    return jnp.clip(values, min=-most, max=most).astype(dtype)


def setup_inputs(seed: int = 0) -> dict:
    keys = jax.random.split(jax.random.key(seed), 6)
    amplitudes = bell_draw(keys[0], (PAIRS, VA, VA), 1.0, 6.0, ((0, 64), (1, 4)), jnp.float32)
    ladder_ints = bell_draw(keys[1], (VA, VA, VA * VA), (VA * VA) ** -0.5, 0.046875, ((0, 4), (2, 64)), jnp.float32)
    cycle_ints = bell_draw(keys[2], (NOCC, VA, NOCC, VA), (NOCC * VA) ** -0.5, 0.125, ((3, 4),), jnp.float32)
    occ_energy = jnp.clip(jax.random.uniform(keys[3], (NOCC,), jnp.float32, -2.0, -0.5), -2.0, -0.5)
    virt_energy = jnp.clip(jax.random.uniform(keys[4], (VA,), jnp.float32, 0.5, 3.0), 0.5, 3.0)
    return dict(amplitudes=amplitudes, ladder_ints=ladder_ints, cycle_ints=cycle_ints, occ_energy=occ_energy, virt_energy=virt_energy)


def reference(amplitudes, ladder_ints, cycle_ints, occ_energy, virt_energy):
    flat_amps = amplitudes.reshape(PAIRS, VA * VA)
    ladder = jnp.dot(flat_amps, ladder_ints.reshape(VA * VA, VA * VA), precision=lax.Precision.HIGHEST, preferred_element_type=jnp.float32).reshape(PAIRS, VA, VA)
    four_amps = amplitudes.reshape(NOCC, NOCC, VA, VA)
    cycle = jnp.einsum("iakc,kjcb->ijab", cycle_ints, four_amps, precision=lax.Precision.HIGHEST).reshape(PAIRS, VA, VA)
    residual = ladder + cycle
    occ_pair = (occ_energy[:, None] + occ_energy[None, :]).reshape(PAIRS)
    denom = virt_energy[None, :, None] + virt_energy[None, None, :] - occ_pair[:, None, None]
    return residual / denom
```

```python
import jax
import jax.numpy as jnp
from jax import lax
from jax.experimental import pallas as pl
from jax.experimental.pallas import tpu as pltpu
from jax.sharding import PartitionSpec as P

F32 = jnp.float32
BF16 = jnp.bfloat16
NY, NZ, NX = 4, 8, 4
PH = 4
CP = 4
ROWS = CP * 8
N_GATHER = 48


def split(v):
    hi = v.astype(BF16)
    lo = (v - hi.astype(F32)).astype(BF16)
    return hi, lo


def dot3(a, b):
    ahi, alo = a
    bhi, blo = b
    out = jnp.dot(ahi, bhi, preferred_element_type=F32)
    out += jnp.dot(ahi, blo, preferred_element_type=F32)
    out += jnp.dot(alo, bhi, preferred_element_type=F32)
    return out


def kernel(
    amps, ints, wts, out,
    raw, gat, vraw, vhi, vlo, wraw, sel, selt, wl_hi, wl_lo, lad, cyc, part, got1, got2, fin,
    lsem, ssem, rsem, asend, arecv,
):
    t = lax.axis_index("tensor")
    x = lax.axis_index("contract")
    h = t % 2
    u = t // 2
    z = u % NZ
    y = u // NZ

    def dev(yy, zz, hh, xx):
        return ((yy * NZ + zz) * 2 + hh, xx)

    sib = dev(y, z, 1 - h, x)

    def ymod(v):
        return (v + NY) % NY

    def zmod(v):
        return (v + NZ) % NZ

    bar = pltpu.get_barrier_semaphore()

    def greet(d):
        pl.semaphore_signal(bar, inc=1, device_id=d, device_id_type=pl.DeviceIdType.MESH)

    greet(sib)
    for dx in range(1, NX):
        greet((t, (x + dx) % NX))

    def greet_step(k, carry):
        uu = (u + k) % 32
        greet((uu * 2 + h, x))
        return carry

    lax.fori_loop(1, 32, greet_step, 0)

    wcopy = pltpu.make_async_copy(wts.at[:, :, pl.ds(h * 16, 16), :], wraw, lsem.at[0])
    acopy = pltpu.make_async_copy(
        amps.at[:, pl.ds(h * 16, 16), :], raw.at[pl.ds(h * 4, 4)], lsem.at[1]
    )
    acopy.start()
    own_cols = pl.multiple_of(h * 256, 256)
    sib_cols = pl.multiple_of((1 - h) * 256, 256)
    vcopies = [
        pltpu.make_async_copy(
            ints.at[pl.ds(h * 16 + q * CP, CP)],
            vraw.at[pl.ds(q * CP, CP), :, pl.ds(own_cols, 256)],
            lsem.at[2 + q],
        )
        for q in range(PH)
    ]
    wcopy.start()
    for c in vcopies:
        c.start()

    pl.semaphore_wait(bar, 31 + 1 + 3)

    sends = []

    def remote(n, src, dst, device):
        c = pltpu.make_async_remote_copy(
            src_ref=src, dst_ref=dst, send_sem=ssem.at[n], recv_sem=rsem.at[n],
            device_id=device, device_id_type=pl.DeviceIdType.MESH,
        )
        c.start()
        sends.append(c)

    def arrive(n, dst):
        pltpu.make_async_remote_copy(
            src_ref=dst, dst_ref=dst, send_sem=ssem.at[n], recv_sem=rsem.at[n],
            device_id=sib, device_id_type=pl.DeviceIdType.MESH,
        ).wait_recv()

    remote(0, amps.at[:, pl.ds((1 - h) * 16, 16), :], raw.at[pl.ds(h * 4, 4)], sib)
    for q in range(PH):
        remote(
            1 + q,
            ints.at[pl.ds((1 - h) * 16 + q * CP, CP)],
            vraw.at[pl.ds(q * CP, CP), :, pl.ds(own_cols, 256)],
            sib,
        )
    acopy.wait()
    arrive(0, raw.at[pl.ds((1 - h) * 4, 4)])

    for c in range(16):
        q, cc = c // CP, c % CP
        gat[q, y, z, cc * 8:(cc + 1) * 8, :] = raw[:, c, :]

    base = 8

    def yz_y(q):
        for dy in range(1, NY):
            remote(base + q * 12 + dy, gat.at[q, y, z], gat.at[q, y, z], dev(ymod(y + dy), z, h, x))

    def yz_y_arrive(q):
        for dy in range(1, NY):
            arrive(base + q * 12 + dy, gat.at[q, ymod(y - dy), z])

    def yz_z(q, s):
        n = base + q * 12 + 4 + 2 * (s - 1)
        ylo, yhi = ((0, 4), (0, 4)) if s < 4 else ((0, 2), (2, 2))
        a = gat.at[q, pl.ds(*ylo), zmod(z - (s - 1))]
        b = gat.at[q, pl.ds(*yhi), zmod(z + (s - 1))]
        remote(n, a, a, dev(y, zmod(z + 1), h, x))
        remote(n + 1, b, b, dev(y, zmod(z - 1), h, x))

    def yz_z_arrive(q, s):
        n = base + q * 12 + 4 + 2 * (s - 1)
        ylo, yhi = ((0, 4), (0, 4)) if s < 4 else ((0, 2), (2, 2))
        arrive(n, gat.at[q, pl.ds(*ylo), zmod(z - s)])
        arrive(n + 1, gat.at[q, pl.ds(*yhi), zmod(z + s)])

    def zy_z(q, s):
        n = base + q * 12 + 2 * (s - 1)
        rlo, rhi = ((0, ROWS), (0, ROWS)) if s < 4 else ((0, ROWS // 2), (ROWS // 2, ROWS // 2))
        a = gat.at[q, y, zmod(z - (s - 1)), pl.ds(*rlo)]
        b = gat.at[q, y, zmod(z + (s - 1)), pl.ds(*rhi)]
        remote(n, a, a, dev(y, zmod(z + 1), h, x))
        remote(n + 1, b, b, dev(y, zmod(z - 1), h, x))

    def zy_z_arrive(q, s):
        n = base + q * 12 + 2 * (s - 1)
        rlo, rhi = ((0, ROWS), (0, ROWS)) if s < 4 else ((0, ROWS // 2), (ROWS // 2, ROWS // 2))
        arrive(n, gat.at[q, y, zmod(z - s), pl.ds(*rlo)])
        arrive(n + 1, gat.at[q, y, zmod(z + s), pl.ds(*rhi)])

    def zy_y(q, s):
        n = base + q * 12 + 8 + 2 * (s - 1)
        zlo, zhi = ((0, 8), (0, 8)) if s < 2 else ((0, 4), (4, 4))
        a = gat.at[q, ymod(y - (s - 1)), pl.ds(*zlo)]
        b = gat.at[q, ymod(y + (s - 1)), pl.ds(*zhi)]
        remote(n, a, a, dev(ymod(y + 1), z, h, x))
        remote(n + 1, b, b, dev(ymod(y - 1), z, h, x))

    def zy_y_arrive(q, s):
        n = base + q * 12 + 8 + 2 * (s - 1)
        zlo, zhi = ((0, 8), (0, 8)) if s < 2 else ((0, 4), (4, 4))
        arrive(n, gat.at[q, ymod(y - s), pl.ds(*zlo)])
        arrive(n + 1, gat.at[q, ymod(y + s), pl.ds(*zhi)])

    def prepare_ints(q):
        vcopies[q].wait()
        arrive(1 + q, vraw.at[pl.ds(q * CP, CP), :, pl.ds(sib_cols, 256)])

        def step(c, carry):
            cc = q * CP + c
            hi, lo = split(vraw[cc])
            at = pl.multiple_of(cc * 128, 128)
            vhi[pl.ds(at, 128), :] = hi
            vlo[pl.ds(at, 128), :] = lo
            return carry

        lax.fori_loop(0, CP, step, 0)

    def prepare_weights():
        wcopy.wait()
        lane = lax.broadcasted_iota(jnp.int32, (256, 128), 1)

        def step(i, acc):
            w = wraw[i].reshape(256, 128)
            shift = (4 * i - 4 * u + 128) % 128
            return jnp.where(lane // 4 == i, pltpu.roll(w, shift, 1), acc)

        sel[...] = lax.fori_loop(0, 16, step, jnp.zeros((256, 128), F32))
        for half in range(2):
            block = jnp.concatenate(
                [sel[pl.ds(half * 8 + c, 16, stride=16), :] for c in range(8)], axis=0
            )
            selt[half] = block.T
            rows = jnp.concatenate(
                [selt.at[half][pl.ds(a, 16, stride=4), :] for a in range(4)], axis=0
            )
            hi, lo = split(rows)
            wl_hi[half] = hi
            wl_lo[half] = lo

    def ladder(q):
        a = jnp.concatenate(
            [gat[q, :, :, c * 8:(c + 1) * 8, :].reshape(256, 128) for c in range(CP)], axis=1
        )
        ahi, alo = split(a)
        for n in range(2):
            cols = slice(n * 256, (n + 1) * 256)
            rows = slice(q * CP * 128, (q + 1) * CP * 128)
            r = dot3((ahi, alo), (vhi[rows, cols], vlo[rows, cols]))
            for m in range(2):
                at = slice((2 * n + m) * 256, (2 * n + m + 1) * 256)
                val = r[:, m * 128:(m + 1) * 128]
                if q == 0:
                    lad[at, :] = val
                else:
                    lad[at, :] += val

    flat = gat.reshape(PH * 32 * ROWS, 128)

    def cycle(half):
        w = (wl_hi[half], wl_lo[half])

        def column(j):
            pieces = []
            for c in range(8):
                q, cc = half * 2 + c // CP, c % CP
                start = ((q * 32 + j // 8) * CP + cc) * 8 + j % 8
                pieces.append(flat[pl.ds(start, 16, stride=2 * ROWS), :])
            return jnp.concatenate(pieces, axis=0)

        for jp in range(8):
            b = jnp.concatenate([column(2 * jp), column(2 * jp + 1)], axis=1)
            r = dot3(w, split(b))
            for m in range(2):
                val = r[:, m * 128:(m + 1) * 128]
                at = slice((2 * jp + m) * 64, (2 * jp + m + 1) * 64)
                if half == 0:
                    cyc[at, :] = val
                else:
                    cyc[at, :] += val

    yz_y(0)
    zy_z(1, 1)
    yz_y(2)
    zy_z(3, 1)
    yz_y_arrive(0)
    yz_z(0, 1)
    zy_z_arrive(1, 1)
    zy_z(1, 2)
    zy_z_arrive(1, 2)
    zy_z(1, 3)
    yz_z_arrive(0, 1)
    yz_z(0, 2)
    zy_z_arrive(1, 3)
    zy_z(1, 4)
    zy_z_arrive(3, 1)
    zy_z(3, 2)
    yz_y_arrive(2)
    prepare_ints(0)
    zy_z_arrive(1, 4)
    zy_y(1, 1)
    yz_z_arrive(0, 2)
    yz_z(0, 3)
    zy_z_arrive(3, 2)
    zy_z(3, 3)
    yz_z(2, 1)
    prepare_weights()
    yz_z_arrive(0, 3)
    yz_z(0, 4)
    zy_z_arrive(3, 3)
    zy_z(3, 4)
    prepare_ints(1)
    yz_z_arrive(2, 1)
    yz_z(2, 2)
    zy_z_arrive(3, 4)
    zy_y(3, 1)
    zy_y_arrive(1, 1)
    zy_y(1, 2)
    yz_z_arrive(0, 4)
    ladder(0)
    prepare_ints(2)
    yz_z_arrive(2, 2)
    yz_z(2, 3)
    zy_y_arrive(1, 2)
    ladder(1)
    zy_y_arrive(3, 1)
    zy_y(3, 2)
    yz_z_arrive(2, 3)
    yz_z(2, 4)
    cycle(0)
    prepare_ints(3)
    zy_y_arrive(3, 2)
    ladder(3)
    yz_z_arrive(2, 4)
    ladder(2)
    cycle(1)

    def assemble(s):
        for jh in range(2):
            for a in range(4):
                l = lad[pl.ds(a * 256 + 8 * jh + s, 16, stride=16), :]
                c = cyc[pl.ds((jh * 8 + s) * 64 + a * 16, 16), :]
                part[pl.ds((s * 32 + jh * 16) * 4 + a, 16, stride=4), :] = l + c

    for s in range(8):
        assemble(s)

    n_core = 5
    sib_rows = pl.multiple_of((1 - h) * 512, 512)
    own_rows = pl.multiple_of(h * 512, 512)
    remote(n_core, part.at[pl.ds(sib_rows, 512), :], got1, sib)
    arrive(n_core, got1)
    got1[...] = got1[...] + part[pl.ds(own_rows, 512), :]

    n_x = base + 48
    for dx in range(1, NX):
        to = (x + dx) % NX
        remote(n_x + dx, got1.at[pl.ds(pl.multiple_of(to * 128, 128), 128), :], got2.at[dx - 1], (t, to))
    for dx in range(1, NX):
        arrive(n_x + dx, got2.at[dx - 1])
    mine = got1[pl.ds(pl.multiple_of(x * 128, 128), 128), :]
    fin[...] = mine + got2[0] + got2[1] + got2[2]

    def place(uu):
        return ((uu % 2) * 16 + uu // 2) * 4

    def a2a(k, to, frm):
        return pltpu.make_async_remote_copy(
            src_ref=fin.at[pl.ds(place(to), 4), :],
            dst_ref=out.at[pl.ds(frm * 4, 4), :],
            send_sem=asend.at[k], recv_sem=arecv.at[k],
            device_id=(to * 2 + h, x), device_id_type=pl.DeviceIdType.MESH,
        )

    def a2a_start(k, carry):
        a2a(k, (u + k) % 32, u).start()
        return carry

    lax.fori_loop(1, 32, a2a_start, 0)
    keep = pltpu.make_async_copy(fin.at[pl.ds(place(u), 4), :], out.at[pl.ds(u * 4, 4), :], lsem.at[6])
    keep.start()
    keep.wait()

    def a2a_wait(k, carry):
        a2a(k, (u + k) % 32, (u - k + 32) % 32).wait_recv()
        return carry

    lax.fori_loop(1, 32, a2a_wait, 0)

    def a2a_sent(k, carry):
        a2a(k, (u + k) % 32, u).wait_send()
        return carry

    lax.fori_loop(1, 32, a2a_sent, 0)
    for c in sends:
        c.wait_send()


def body(amplitudes, ladder_ints, cycle_ints, occ_energy, virt_energy):
    wts = jnp.transpose(cycle_ints, (0, 2, 3, 1))
    n_sem = 8 + 48 + 4
    summed = pl.pallas_call(
        kernel,
        out_shape=jax.ShapeDtypeStruct((128, 128), F32),
        in_specs=[pl.BlockSpec(memory_space=pl.ANY)] * 3,
        out_specs=pl.BlockSpec(memory_space=pltpu.VMEM),
        scratch_shapes=[
            pltpu.VMEM((8, 16, 128), F32),
            pltpu.VMEM((PH, NY, NZ, ROWS, 128), F32),
            pltpu.VMEM((16, 128, 512), F32),
            pltpu.VMEM((2048, 512), BF16),
            pltpu.VMEM((2048, 512), BF16),
            pltpu.VMEM((16, 16, 16, 128), F32),
            pltpu.VMEM((256, 128), F32),
            pltpu.VMEM((2, 128, 128), F32),
            pltpu.VMEM((2, 64, 128), BF16),
            pltpu.VMEM((2, 64, 128), BF16),
            pltpu.VMEM((1024, 128), F32),
            pltpu.VMEM((1024, 128), F32),
            pltpu.VMEM((1024, 128), F32),
            pltpu.VMEM((512, 128), F32),
            pltpu.VMEM((3, 128, 128), F32),
            pltpu.VMEM((128, 128), F32),
            pltpu.SemaphoreType.DMA((8,)),
            pltpu.SemaphoreType.DMA((n_sem,)),
            pltpu.SemaphoreType.DMA((n_sem,)),
            pltpu.SemaphoreType.DMA((32,)),
            pltpu.SemaphoreType.DMA((32,)),
        ],
        compiler_params=pltpu.CompilerParams(
            collective_id=0, has_side_effects=True, vmem_limit_bytes=48 * 1024 * 1024
        ),
        cost_estimate=pl.CostEstimate(flops=2_000_000_000, bytes_accessed=8_000_000, transcendentals=0),
        name="ladder_cycle",
    )(amplitudes, ladder_ints, wts)
    nocc = occ_energy.shape[0]
    pair = lax.axis_index("tensor") * NX + lax.axis_index("contract")
    occ_ids = jnp.arange(nocc, dtype=jnp.int32)
    occ_i = jnp.sum(jnp.where(occ_ids == pair // nocc, occ_energy, 0.0))
    occ_j = jnp.sum(jnp.where(occ_ids == pair % nocc, occ_energy, 0.0))
    denom = virt_energy[:, None] + virt_energy[None, :] - (occ_i + occ_j)
    return (summed / denom)[None]


def solution(mesh):
    in_specs = (
        P("tensor", "contract", None),
        P("contract", None, "tensor"),
        P(None, None, None, "contract"),
        P(),
        P(),
    )
    out_specs = P(("tensor", "contract"), None, None)
    return jax.shard_map(body, mesh=mesh, in_specs=in_specs, out_specs=out_specs, check_vma=False)
```

```python
import jax
import jax.numpy as jnp
from jax import lax
from jax.experimental import pallas as pl
from jax.experimental.pallas import tpu as pltpu
from jax.sharding import PartitionSpec as P

F32 = jnp.float32
BF16 = jnp.bfloat16
NY, NZ, NX = 4, 8, 4
PH = 4
CP = 4
PHASES = (("yz", 0, 4), ("zy", 4, 6), ("zy", 10, 6))
ORDER = (
    "C0", "A0", "B0", "v0", "C1", "A1", "B1", "w", "A2", "C2", "B2", "A3",
    "A4", "B3", "C3", "A5", "B4", "v1", "A6", "A7", "B5", "C4", "v2", "A8",
    "B6", "A9", "B7", "v3", "C5", "B8", "B9", "mC", "A10", "mA", "B10", "mB",
)


def split(v):
    hi = v.astype(BF16)
    lo = (v - hi.astype(F32)).astype(BF16)
    return hi, lo


def dot3(a, b):
    ahi, alo = a
    bhi, blo = b
    out = jnp.dot(ahi, bhi, preferred_element_type=F32)
    out += jnp.dot(ahi, blo, preferred_element_type=F32)
    out += jnp.dot(alo, bhi, preferred_element_type=F32)
    return out


def kernel(
    amps, ints, wts, occ_in, virt_in, out,
    raw, gat_c, gat_a, gat_b, vraw, vhi, vlo, wraw, sel, selt, wl_hi, wl_lo, lad, cyc, part, got1, got2, fin, land, occ, virt, den,
    lsem, ssem, rsem, asend, arecv,
):
    gats = (gat_c, gat_a, gat_b)
    t = lax.axis_index("tensor")
    x = lax.axis_index("contract")
    h = t % 2
    u = t // 2
    z = u % NZ
    y = u // NZ

    def dev(yy, zz, hh, xx):
        return ((yy * NZ + zz) * 2 + hh, xx)

    sib = dev(y, z, 1 - h, x)

    def ymod(v):
        return (v + NY) % NY

    def zmod(v):
        return (v + NZ) % NZ

    bar = pltpu.get_barrier_semaphore()

    def greet(d):
        pl.semaphore_signal(bar, inc=1, device_id=d, device_id_type=pl.DeviceIdType.MESH)

    greet(sib)
    for dx in range(1, NX):
        greet((t, (x + dx) % NX))

    for dy in range(1, NY):
        greet(dev(ymod(y + dy), z, h, x))
    for dz in (1, 2, -1, -2):
        greet(dev(y, zmod(z + dz), h, x))

    wcopy = pltpu.make_async_copy(wts.at[:, :, pl.ds(h * 16, 16), :], wraw, lsem.at[0])
    acopy = pltpu.make_async_copy(
        amps.at[:, pl.ds(h * 16, 16), :], raw.at[pl.ds(h * 4, 4)], lsem.at[1]
    )
    acopy.start()
    own_cols = pl.multiple_of(h * 256, 256)
    sib_cols = pl.multiple_of((1 - h) * 256, 256)
    vcopies = [
        pltpu.make_async_copy(
            ints.at[pl.ds(h * 16 + q * CP, CP)],
            vraw.at[pl.ds(q * CP, CP), :, pl.ds(own_cols, 256)],
            lsem.at[2 + q],
        )
        for q in range(PH)
    ]
    wcopy.start()
    ecopies = [
        pltpu.make_async_copy(occ_in, occ, lsem.at[7]),
        pltpu.make_async_copy(virt_in, virt, lsem.at[8]),
    ]
    for c in ecopies:
        c.start()
    for c in vcopies:
        c.start()

    pl.semaphore_wait(bar, 1 + 3 + 3 + 4)

    sends = []

    def remote(n, src, dst, device):
        c = pltpu.make_async_remote_copy(
            src_ref=src, dst_ref=dst, send_sem=ssem.at[n], recv_sem=rsem.at[n],
            device_id=device, device_id_type=pl.DeviceIdType.MESH,
        )
        c.start()
        sends.append(c)

    def arrive(n, dst):
        pltpu.make_async_remote_copy(
            src_ref=dst, dst_ref=dst, send_sem=ssem.at[n], recv_sem=rsem.at[n],
            device_id=sib, device_id_type=pl.DeviceIdType.MESH,
        ).wait_recv()

    remote(0, amps.at[:, pl.ds((1 - h) * 16, 16), :], raw.at[pl.ds(h * 4, 4)], sib)
    for q in range(PH):
        remote(
            1 + q,
            ints.at[pl.ds((1 - h) * 16 + q * CP, CP)],
            vraw.at[pl.ds(q * CP, CP), :, pl.ds(own_cols, 256)],
            sib,
        )
    acopy.wait()
    arrive(0, raw.at[pl.ds((1 - h) * 4, 4)])

    for gat, (_, c0, nc) in zip(gats, PHASES):
        for c in range(nc):
            gat[y, z, c * 8:(c + 1) * 8, :] = raw[:, c0 + c, :]

    ids = {}

    def sem(key):
        return ids.setdefault(key, 8 + len(ids))

    def at_z(d):
        return (z + d + NZ) % NZ

    def at_y(d):
        return (y + d + NY) % NY

    def yz(q, k):
        gat = gats[q]
        if k > 0:
            if k == 1:
                for dy in range(1, NY):
                    arrive(sem((q, "y", dy)), gat.at[at_y(-dy), z])
            else:
                lo, hi = ((0, 4), (0, 4)) if k < 5 else ((0, 2), (2, 2))
                arrive(sem((q, "z+", k)), gat.at[pl.ds(*lo), at_z(-(k - 1))])
                arrive(sem((q, "z-", k)), gat.at[pl.ds(*hi), at_z(k - 1)])
        if k == 0:
            for dy in range(1, NY):
                remote(sem((q, "y", dy)), gat.at[y, z], gat.at[y, z], dev(at_y(dy), z, h, x))
        elif k < 5:
            lo, hi = ((0, 4), (0, 4)) if k < 4 else ((0, 2), (2, 2))
            a = gat.at[pl.ds(*lo), at_z(-(k - 1))]
            b = gat.at[pl.ds(*hi), at_z(k - 1)]
            remote(sem((q, "z+", k + 1)), a, a, dev(y, at_z(1), h, x))
            remote(sem((q, "z-", k + 1)), b, b, dev(y, at_z(-1), h, x))

    def zy(q, k):
        gat = gats[q]
        rows = PHASES[q][2] * 8
        half = PHASES[q][2] // 2 * 8
        cut = {1: pl.ds(0, half), -1: pl.ds(half, rows - half)}

        def own_z(d):
            remote(sem((q, "z", d)), gat.at[y, z], gat.at[y, z], dev(y, at_z(d), h, x))

        def got_z(d):
            if abs(d) < 4:
                arrive(sem((q, "z", -d)), gat.at[y, at_z(d)])
            else:
                for sign in (1, -1):
                    arrive(sem((q, "z4", sign)), gat.at[y, at_z(4), cut[sign]])

        def forward_z(sign):
            b = gat.at[y, at_z(-2 * sign)]
            remote(sem((q, "z", 3 * sign)), b, b, dev(y, at_z(sign), h, x))
            c = gat.at[y, at_z(-2 * sign), cut[sign]]
            remote(sem((q, "z4", sign)), c, c, dev(y, at_z(2 * sign), h, x))

        def y1(d):
            for sign in (1, -1):
                b = gat.at[y, at_z(d)]
                remote(sem((q, "y1", d, sign)), b, b, dev(at_y(sign), z, h, x))

        def got_y1(d):
            for sign in (1, -1):
                arrive(sem((q, "y1", d, sign)), gat.at[at_y(-sign), at_z(d)])

        def y2(d, sign):
            b = gat.at[at_y(-sign), at_z(d)]
            remote(sem((q, "y2", d)), b, b, dev(at_y(sign), z, h, x))

        def got_y2(d):
            arrive(sem((q, "y2", d)), gat.at[at_y(2), at_z(d)])

        if k == 0:
            for d in (1, -1, 2, -2):
                own_z(d)
            y1(0)
        elif k == 1:
            got_z(1); got_z(-1)
            y1(1); y1(-1)
        elif k == 2:
            got_z(2); got_z(-2)
            forward_z(1); forward_z(-1)
            y1(2); y1(-2)
        elif k == 3:
            got_y1(0)
            y2(0, 1)
        elif k == 4:
            got_z(3); got_z(-3)
            y1(3); y1(-3)
        elif k == 5:
            got_y1(1); got_y1(-1)
            y2(1, 1); y2(-1, -1)
        elif k == 6:
            got_z(4)
            y1(4)
        elif k == 7:
            got_y1(2); got_y1(-2)
            y2(-2, 1); y2(2, -1)
        elif k == 8:
            got_y1(3); got_y1(-3)
            y2(3, 1); y2(-3, -1)
        elif k == 9:
            got_y1(4)
            y2(4, -1)
        elif k == 10:
            for d in (0, 1, -1, -2, 2, 3, -3, 4):
                got_y2(d)

    def prepare_ints(q):
        vcopies[q].wait()
        arrive(1 + q, vraw.at[pl.ds(q * CP, CP), :, pl.ds(sib_cols, 256)])

        def step(c, carry):
            cc = q * CP + c
            hi, lo = split(vraw[cc])
            at = pl.multiple_of(cc * 128, 128)
            vhi[pl.ds(at, 128), :] = hi
            vlo[pl.ds(at, 128), :] = lo
            return carry

        lax.fori_loop(0, CP, step, 0)

    def prepare_energies():
        for c in ecopies:
            c.wait()
        pair = t * NX + x
        who = lax.broadcasted_iota(jnp.int32, (1, 16), 1)
        o = occ[...]
        o = jnp.where(who == pair // 16, o, 0.0) + jnp.where(who == pair % 16, o, 0.0)
        v = jnp.broadcast_to(virt[...], (128, 128))
        den[...] = v.T + v - jnp.sum(o, axis=1, keepdims=True)

    def prepare_weights():
        wcopy.wait()
        lane = lax.broadcasted_iota(jnp.int32, (256, 128), 1)

        def step(i, acc):
            w = wraw[i].reshape(256, 128)
            shift = (4 * i - 4 * u + 128) % 128
            return jnp.where(lane // 4 == i, pltpu.roll(w, shift, 1), acc)

        sel[...] = lax.fori_loop(0, 16, step, jnp.zeros((256, 128), F32))
        for q, (_, c0, nc) in enumerate(PHASES):
            block = jnp.concatenate(
                [sel[pl.ds(c0 + c, 16, stride=16), :] for c in range(nc)], axis=0
            )
            block = jnp.concatenate([block, jnp.zeros((128 - nc * 16, 128), F32)], axis=0)
            selt[q] = block.T
            rows = jnp.concatenate(
                [selt.at[q][pl.ds(a, 16, stride=4), :] for a in range(4)], axis=0
            )
            hi, lo = split(rows)
            wl_hi[q] = hi
            wl_lo[q] = lo

    def ladder(q, first):
        gat = gats[q]
        _, c0, nc = PHASES[q]
        a = jnp.concatenate(
            [gat[:, :, c * 8:(c + 1) * 8, :].reshape(256, 128) for c in range(nc)], axis=1
        )
        ahi, alo = split(a)
        for n in range(2):
            cols = slice(n * 256, (n + 1) * 256)
            rows = slice(c0 * 128, (c0 + nc) * 128)
            r = dot3((ahi, alo), (vhi[rows, cols], vlo[rows, cols]))
            for m in range(2):
                at = slice((2 * n + m) * 256, (2 * n + m + 1) * 256)
                val = r[:, m * 128:(m + 1) * 128]
                if first:
                    lad[at, :] = val
                else:
                    lad[at, :] += val

    def cycle(q, first):
        _, c0, nc = PHASES[q]
        flat = gats[q].reshape(32 * nc * 8, 128)
        w = (wl_hi[q, :, 0:nc * 16], wl_lo[q, :, 0:nc * 16])

        def column(j):
            return jnp.concatenate(
                [
                    flat[pl.ds(((j // 8) * nc + c) * 8 + j % 8, 16, stride=2 * nc * 8), :]
                    for c in range(nc)
                ],
                axis=0,
            )

        for jp in range(8):
            b = jnp.concatenate([column(2 * jp), column(2 * jp + 1)], axis=1)
            r = dot3(w, split(b))
            for m in range(2):
                val = r[:, m * 128:(m + 1) * 128]
                at = slice((2 * jp + m) * 64, (2 * jp + m + 1) * 64)
                if first:
                    cyc[at, :] = val
                else:
                    cyc[at, :] += val

    first = True
    for step in ORDER:
        if step == "w":
            prepare_weights()
            prepare_energies()
        elif step[0] == "v":
            prepare_ints(int(step[1:]))
        elif step[0] == "m":
            q = "CAB".index(step[1])
            ladder(q, first)
            cycle(q, first)
            first = False
        else:
            q = "CAB".index(step[0])
            (yz if PHASES[q][0] == "yz" else zy)(q, int(step[1:]))

    def assemble(s):
        for jh in range(2):
            for a in range(4):
                l = lad[pl.ds(a * 256 + 8 * jh + s, 16, stride=16), :]
                c = cyc[pl.ds((jh * 8 + s) * 64 + a * 16, 16), :]
                part[pl.ds((s * 32 + jh * 16) * 4 + a, 16, stride=4), :] = l + c

    for s in range(8):
        assemble(s)

    n_core = 5
    sib_rows = pl.multiple_of((1 - h) * 512, 512)
    own_rows = pl.multiple_of(h * 512, 512)
    remote(n_core, part.at[pl.ds(sib_rows, 512), :], got1, sib)
    arrive(n_core, got1)
    got1[...] = got1[...] + part[pl.ds(own_rows, 512), :]

    n_x = 8 + len(ids)
    for dx in range(1, NX):
        to = (x + dx) % NX
        remote(n_x + dx, got1.at[pl.ds(pl.multiple_of(to * 128, 128), 128), :], got2.at[dx - 1], (t, to))
    for dx in range(1, NX):
        arrive(n_x + dx, got2.at[dx - 1])
    mine = got1[pl.ds(pl.multiple_of(x * 128, 128), 128), :]
    fin[...] = mine + got2[0] + got2[1] + got2[2]

    def place(uu):
        return ((uu % 2) * 16 + uu // 2) * 4

    def a2a(k, to, frm):
        return pltpu.make_async_remote_copy(
            src_ref=fin.at[pl.ds(place(to), 4), :],
            dst_ref=land.at[pl.ds(frm * 4, 4), :],
            send_sem=asend.at[k], recv_sem=arecv.at[k],
            device_id=(to * 2 + h, x), device_id_type=pl.DeviceIdType.MESH,
        )

    def a2a_start(k, carry):
        a2a(k, (u + k) % 32, u).start()
        return carry

    lax.fori_loop(1, 32, a2a_start, 0)
    keep = pltpu.make_async_copy(fin.at[pl.ds(place(u), 4), :], land.at[pl.ds(u * 4, 4), :], lsem.at[6])
    keep.start()
    keep.wait()

    def a2a_wait(k, carry):
        a2a(k, (u + k) % 32, (u - k + 32) % 32).wait_recv()
        return carry

    lax.fori_loop(1, 32, a2a_wait, 0)
    out[...] = land[...] / den[...]

    def a2a_sent(k, carry):
        a2a(k, (u + k) % 32, u).wait_send()
        return carry

    lax.fori_loop(1, 32, a2a_sent, 0)
    for c in sends:
        c.wait_send()


def body(amplitudes, ladder_ints, cycle_ints, occ_energy, virt_energy):
    wts = jnp.transpose(cycle_ints, (0, 2, 3, 1))
    n_sem = 120
    summed = pl.pallas_call(
        kernel,
        out_shape=jax.ShapeDtypeStruct((128, 128), F32),
        in_specs=[pl.BlockSpec(memory_space=pl.ANY)] * 5,
        out_specs=pl.BlockSpec(memory_space=pltpu.VMEM),
        scratch_shapes=[
            pltpu.VMEM((8, 16, 128), F32),
            *[pltpu.VMEM((NY, NZ, nc * 8, 128), F32) for _, _, nc in PHASES],
            pltpu.VMEM((16, 128, 512), F32),
            pltpu.VMEM((2048, 512), BF16),
            pltpu.VMEM((2048, 512), BF16),
            pltpu.VMEM((16, 16, 16, 128), F32),
            pltpu.VMEM((256, 128), F32),
            pltpu.VMEM((3, 128, 128), F32),
            pltpu.VMEM((3, 64, 128), BF16),
            pltpu.VMEM((3, 64, 128), BF16),
            pltpu.VMEM((1024, 128), F32),
            pltpu.VMEM((1024, 128), F32),
            pltpu.VMEM((1024, 128), F32),
            pltpu.VMEM((512, 128), F32),
            pltpu.VMEM((3, 128, 128), F32),
            pltpu.VMEM((128, 128), F32),
            pltpu.VMEM((128, 128), F32),
            pltpu.VMEM((1, 16), F32),
            pltpu.VMEM((1, 128), F32),
            pltpu.VMEM((128, 128), F32),
            pltpu.SemaphoreType.DMA((9,)),
            pltpu.SemaphoreType.DMA((n_sem,)),
            pltpu.SemaphoreType.DMA((n_sem,)),
            pltpu.SemaphoreType.DMA((32,)),
            pltpu.SemaphoreType.DMA((32,)),
        ],
        compiler_params=pltpu.CompilerParams(
            collective_id=0, has_side_effects=True, vmem_limit_bytes=60 * 1024 * 1024
        ),
        cost_estimate=pl.CostEstimate(flops=2_000_000_000, bytes_accessed=8_000_000, transcendentals=0),
        name="ladder_cycle",
    )(amplitudes, ladder_ints, wts, occ_energy.reshape(1, -1), virt_energy.reshape(1, -1))
    return summed[None]


def solution(mesh):
    in_specs = (
        P("tensor", "contract", None),
        P("contract", None, "tensor"),
        P(None, None, None, "contract"),
        P(),
        P(),
    )
    out_specs = P(("tensor", "contract"), None, None)
    return jax.shard_map(body, mesh=mesh, in_specs=in_specs, out_specs=out_specs, check_vma=False)
```

```python
import jax
import jax.numpy as jnp
from jax import lax
from jax.experimental import pallas as pl
from jax.experimental.pallas import tpu as pltpu
from jax.sharding import PartitionSpec as P

F32 = jnp.float32
BF16 = jnp.bfloat16
NY, NZ, NX = 4, 8, 4
PH = 4
CP = 4
PHASES = (("yz", 0, 4), ("zy", 4, 7), ("zy", 11, 5))
ORDER = (
    "C0", "B0", "A0", "w", "B1", "B3", "C1", "A1", "B2", "A2", "B5", "C20",
    "C21", "B4", "B6", "A4", "v0", "v3", "C30", "A6", "C31", "v1", "B7", "B8",
    "B9", "C40", "A8", "A3", "v2", "A9", "C41", "A7", "A5", "Bt", "mB", "C5",
    "mC", "At", "mA",
)


def split(v):
    hi = v.astype(BF16)
    lo = (v - hi.astype(F32)).astype(BF16)
    return hi, lo


def dot3(a, b):
    ahi, alo = a
    bhi, blo = b
    out = jnp.dot(ahi, bhi, preferred_element_type=F32)
    out += jnp.dot(ahi, blo, preferred_element_type=F32)
    out += jnp.dot(alo, bhi, preferred_element_type=F32)
    return out


def kernel(
    amps, ints, wts, occ_in, virt_in, out,
    raw, gat_c, gat_a, gat_b, vraw, vhi, vlo, wraw, sel, selt, wl_hi, wl_lo, lad, cyc, part, got1, got2, fin, land, occ, virt, den,
    lsem, ssem, rsem, asend, arecv,
):
    gats = (gat_c, gat_a, gat_b)
    t = lax.axis_index("tensor")
    x = lax.axis_index("contract")
    h = t % 2
    u = t // 2
    z = u % NZ
    y = u // NZ

    def dev(yy, zz, hh, xx):
        return ((yy * NZ + zz) * 2 + hh, xx)

    sib = dev(y, z, 1 - h, x)

    def ymod(v):
        return (v + NY) % NY

    def zmod(v):
        return (v + NZ) % NZ

    bar = pltpu.get_barrier_semaphore()

    def greet(d):
        pl.semaphore_signal(bar, inc=1, device_id=d, device_id_type=pl.DeviceIdType.MESH)

    greet(sib)
    for dx in range(1, NX):
        greet((t, (x + dx) % NX))

    for dy in range(1, NY):
        greet(dev(ymod(y + dy), z, h, x))
    for dz in (1, 2, -1, -2):
        greet(dev(y, zmod(z + dz), h, x))

    wcopy = pltpu.make_async_copy(wts.at[:, :, pl.ds(h * 16, 16), :], wraw, lsem.at[0])
    acopy = pltpu.make_async_copy(
        amps.at[:, pl.ds(h * 16, 16), :], raw.at[pl.ds(h * 4, 4)], lsem.at[1]
    )
    acopy.start()
    own_cols = pl.multiple_of(h * 256, 256)
    sib_cols = pl.multiple_of((1 - h) * 256, 256)
    vcopies = [
        pltpu.make_async_copy(
            ints.at[pl.ds(h * 16 + q * CP, CP)],
            vraw.at[pl.ds(q * CP, CP), :, pl.ds(own_cols, 256)],
            lsem.at[2 + q],
        )
        for q in range(PH)
    ]
    wcopy.start()
    ecopies = [
        pltpu.make_async_copy(occ_in, occ, lsem.at[7]),
        pltpu.make_async_copy(virt_in, virt, lsem.at[8]),
    ]
    for c in ecopies:
        c.start()
    for c in vcopies:
        c.start()

    pl.semaphore_wait(bar, 1 + 3 + 3 + 4)

    sends = []

    def remote(n, src, dst, device):
        c = pltpu.make_async_remote_copy(
            src_ref=src, dst_ref=dst, send_sem=ssem.at[n], recv_sem=rsem.at[n],
            device_id=device, device_id_type=pl.DeviceIdType.MESH,
        )
        c.start()
        sends.append(c)

    def arrive(n, dst):
        pltpu.make_async_remote_copy(
            src_ref=dst, dst_ref=dst, send_sem=ssem.at[n], recv_sem=rsem.at[n],
            device_id=sib, device_id_type=pl.DeviceIdType.MESH,
        ).wait_recv()

    remote(0, amps.at[:, pl.ds((1 - h) * 16, 16), :], raw.at[pl.ds(h * 4, 4)], sib)
    for q in range(PH):
        remote(
            1 + q,
            ints.at[pl.ds((1 - h) * 16 + q * CP, CP)],
            vraw.at[pl.ds(q * CP, CP), :, pl.ds(own_cols, 256)],
            sib,
        )
    acopy.wait()
    arrive(0, raw.at[pl.ds((1 - h) * 4, 4)])

    for gat, (_, c0, nc) in zip(gats, PHASES):
        for c in range(nc):
            gat[y, z, c * 8:(c + 1) * 8, :] = raw[:, c0 + c, :]

    ids = {}

    def sem(key):
        return ids.setdefault(key, 8 + len(ids))

    def at_z(d):
        return (z + d + NZ) % NZ

    def at_y(d):
        return (y + d + NY) % NY

    def yz(q, k, pieces):
        gat = gats[q]

        def group(p, d):
            return gat.at[pl.ds(2 * p, 2), at_z(d)]

        def last(p, sign, step):
            return step < 4 or (p == 0) == (sign == 1)

        if k == 0:
            for dy in range(1, NY):
                remote(sem((q, "y", dy)), gat.at[y, z], gat.at[y, z], dev(at_y(dy), z, h, x))
            return
        if k == 1:
            for dy in range(1, NY):
                arrive(sem((q, "y", dy)), gat.at[at_y(-dy), z])
        for p in pieces:
            if k > 1:
                for sign in (1, -1):
                    if last(p, sign, k - 1):
                        arrive(sem((q, "z", k - 1, sign, p)), group(p, -sign * (k - 1)))
            if k < 5:
                for sign in (1, -1):
                    if last(p, sign, k):
                        b = group(p, -sign * (k - 1))
                        remote(sem((q, "z", k, sign, p)), b, b, dev(y, at_z(sign), h, x))

    def zy(q, k):
        gat = gats[q]
        rows = PHASES[q][2] * 8
        half = PHASES[q][2] // 2 * 8
        cut = {1: pl.ds(0, half), -1: pl.ds(half, rows - half)}

        def own_z(d):
            remote(sem((q, "z", d)), gat.at[y, z], gat.at[y, z], dev(y, at_z(d), h, x))

        def got_z(d):
            if abs(d) < 4:
                arrive(sem((q, "z", -d)), gat.at[y, at_z(d)])
            else:
                for sign in (1, -1):
                    arrive(sem((q, "z4", sign)), gat.at[y, at_z(4), cut[sign]])

        def forward_z(sign):
            b = gat.at[y, at_z(-2 * sign)]
            remote(sem((q, "z", 3 * sign)), b, b, dev(y, at_z(sign), h, x))
            c = gat.at[y, at_z(-2 * sign), cut[sign]]
            remote(sem((q, "z4", sign)), c, c, dev(y, at_z(2 * sign), h, x))

        def y1(d):
            for sign in (1, -1):
                b = gat.at[y, at_z(d)]
                remote(sem((q, "y1", d, sign)), b, b, dev(at_y(sign), z, h, x))

        def got_y1(d):
            for sign in (1, -1):
                arrive(sem((q, "y1", d, sign)), gat.at[at_y(-sign), at_z(d)])

        def y2(d, sign):
            b = gat.at[at_y(-sign), at_z(d)]
            remote(sem((q, "y2", d)), b, b, dev(at_y(sign), z, h, x))

        def got_y2(d):
            arrive(sem((q, "y2", d)), gat.at[at_y(2), at_z(d)])

        if k == 0:
            for d in (1, -1, 2, -2):
                own_z(d)
            y1(0)
        elif k == 1:
            got_z(1); got_z(-1)
            y1(1); y1(-1)
        elif k == 2:
            got_z(2); got_z(-2)
            forward_z(1); forward_z(-1)
            y1(2); y1(-2)
        elif k == 3:
            got_y1(0)
            y2(0, 1)
        elif k == 4:
            got_z(3); got_z(-3)
            y1(3); y1(-3)
        elif k == 5:
            got_y1(1); got_y1(-1)
            y2(1, 1); y2(-1, -1)
        elif k == 6:
            got_z(4)
            y1(4)
        elif k == 7:
            got_y1(2); got_y1(-2)
            y2(-2, 1); y2(2, -1)
        elif k == 8:
            got_y1(3); got_y1(-3)
            y2(3, 1); y2(-3, -1)
        elif k == 9:
            got_y1(4)
            y2(4, -1)
        elif k == 10:
            for d in (0, 1, -1, -2, 2, 3, -3, 4):
                got_y2(d)

    def prepare_ints(q):
        vcopies[q].wait()
        arrive(1 + q, vraw.at[pl.ds(q * CP, CP), :, pl.ds(sib_cols, 256)])

        def step(c, carry):
            cc = q * CP + c
            hi, lo = split(vraw[cc])
            at = pl.multiple_of(cc * 128, 128)
            vhi[pl.ds(at, 128), :] = hi
            vlo[pl.ds(at, 128), :] = lo
            return carry

        lax.fori_loop(0, CP, step, 0)

    def prepare_energies():
        for c in ecopies:
            c.wait()
        pair = t * NX + x
        who = lax.broadcasted_iota(jnp.int32, (1, 16), 1)
        o = occ[...]
        o = jnp.where(who == pair // 16, o, 0.0) + jnp.where(who == pair % 16, o, 0.0)
        v = jnp.broadcast_to(virt[...], (128, 128))
        den[...] = v.T + v - jnp.sum(o, axis=1, keepdims=True)

    def prepare_weights():
        wcopy.wait()
        lane = lax.broadcasted_iota(jnp.int32, (256, 128), 1)

        def step(i, acc):
            w = wraw[i].reshape(256, 128)
            shift = (4 * i - 4 * u + 128) % 128
            return jnp.where(lane // 4 == i, pltpu.roll(w, shift, 1), acc)

        sel[...] = lax.fori_loop(0, 16, step, jnp.zeros((256, 128), F32))
        for q, (_, c0, nc) in enumerate(PHASES):
            block = jnp.concatenate(
                [sel[pl.ds(c0 + c, 16, stride=16), :] for c in range(nc)], axis=0
            )
            block = jnp.concatenate([block, jnp.zeros((128 - nc * 16, 128), F32)], axis=0)
            selt[q] = block.T
            rows = jnp.concatenate(
                [selt.at[q][pl.ds(a, 16, stride=4), :] for a in range(4)], axis=0
            )
            hi, lo = split(rows)
            wl_hi[q] = hi
            wl_lo[q] = lo

    def ladder(q, first):
        gat = gats[q]
        _, c0, nc = PHASES[q]
        a = jnp.concatenate(
            [gat[:, :, c * 8:(c + 1) * 8, :].reshape(256, 128) for c in range(nc)], axis=1
        )
        ahi, alo = split(a)
        for n in range(2):
            cols = slice(n * 256, (n + 1) * 256)
            rows = slice(c0 * 128, (c0 + nc) * 128)
            r = dot3((ahi, alo), (vhi[rows, cols], vlo[rows, cols]))
            for m in range(2):
                at = slice((2 * n + m) * 256, (2 * n + m + 1) * 256)
                val = r[:, m * 128:(m + 1) * 128]
                if first:
                    lad[at, :] = val
                else:
                    lad[at, :] += val

    def cycle(q, first):
        _, c0, nc = PHASES[q]
        flat = gats[q].reshape(32 * nc * 8, 128)
        w = (wl_hi[q, :, 0:nc * 16], wl_lo[q, :, 0:nc * 16])

        def column(j):
            return jnp.concatenate(
                [
                    flat[pl.ds(((j // 8) * nc + c) * 8 + j % 8, 16, stride=2 * nc * 8), :]
                    for c in range(nc)
                ],
                axis=0,
            )

        for jp in range(8):
            b = jnp.concatenate([column(2 * jp), column(2 * jp + 1)], axis=1)
            r = dot3(w, split(b))
            for m in range(2):
                val = r[:, m * 128:(m + 1) * 128]
                at = slice((2 * jp + m) * 64, (2 * jp + m + 1) * 64)
                if first:
                    cyc[at, :] = val
                else:
                    cyc[at, :] += val

    first = True
    for step in ORDER:
        if step == "w":
            prepare_weights()
            prepare_energies()
        elif step[0] == "v":
            prepare_ints(int(step[1:]))
        elif step[0] == "m":
            q = "CAB".index(step[1])
            ladder(q, first)
            cycle(q, first)
            first = False
        else:
            q = "CAB".index(step[0])
            if PHASES[q][0] == "yz":
                yz(q, int(step[1]), [int(p) for p in step[2:]] or [0, 1])
            else:
                zy(q, 10 if step[1] == "t" else int(step[1:]))

    def assemble(s):
        for jh in range(2):
            for a in range(4):
                l = lad[pl.ds(a * 256 + 8 * jh + s, 16, stride=16), :]
                c = cyc[pl.ds((jh * 8 + s) * 64 + a * 16, 16), :]
                part[pl.ds((s * 32 + jh * 16) * 4 + a, 16, stride=4), :] = l + c

    for s in range(8):
        assemble(s)

    n_core = 5
    sib_rows = pl.multiple_of((1 - h) * 512, 512)
    own_rows = pl.multiple_of(h * 512, 512)
    remote(n_core, part.at[pl.ds(sib_rows, 512), :], got1, sib)
    arrive(n_core, got1)
    got1[...] = got1[...] + part[pl.ds(own_rows, 512), :]

    n_x = 8 + len(ids)
    for dx in range(1, NX):
        to = (x + dx) % NX
        remote(n_x + dx, got1.at[pl.ds(pl.multiple_of(to * 128, 128), 128), :], got2.at[dx - 1], (t, to))
    for dx in range(1, NX):
        arrive(n_x + dx, got2.at[dx - 1])
    mine = got1[pl.ds(pl.multiple_of(x * 128, 128), 128), :]
    fin[...] = mine + got2[0] + got2[1] + got2[2]

    def place(uu):
        return ((uu % 2) * 16 + uu // 2) * 4

    def a2a(k, to, frm):
        return pltpu.make_async_remote_copy(
            src_ref=fin.at[pl.ds(place(to), 4), :],
            dst_ref=land.at[pl.ds(frm * 4, 4), :],
            send_sem=asend.at[k], recv_sem=arecv.at[k],
            device_id=(to * 2 + h, x), device_id_type=pl.DeviceIdType.MESH,
        )

    def a2a_start(k, carry):
        a2a(k, (u + k) % 32, u).start()
        return carry

    lax.fori_loop(1, 32, a2a_start, 0)
    keep = pltpu.make_async_copy(fin.at[pl.ds(place(u), 4), :], land.at[pl.ds(u * 4, 4), :], lsem.at[6])
    keep.start()
    keep.wait()

    def a2a_wait(k, carry):
        a2a(k, (u + k) % 32, (u - k + 32) % 32).wait_recv()
        return carry

    lax.fori_loop(1, 32, a2a_wait, 0)
    out[...] = land[...] / den[...]

    def a2a_sent(k, carry):
        a2a(k, (u + k) % 32, u).wait_send()
        return carry

    lax.fori_loop(1, 32, a2a_sent, 0)
    for c in sends:
        c.wait_send()


def body(amplitudes, ladder_ints, cycle_ints, occ_energy, virt_energy):
    wts = jnp.transpose(cycle_ints, (0, 2, 3, 1))
    n_sem = 120
    summed = pl.pallas_call(
        kernel,
        out_shape=pltpu.VMEM((128, 128), F32),
        in_specs=[pl.BlockSpec(memory_space=pl.ANY)] * 5,
        out_specs=pl.BlockSpec(memory_space=pltpu.VMEM),
        scratch_shapes=[
            pltpu.VMEM((8, 16, 128), F32),
            *[pltpu.VMEM((NY, NZ, nc * 8, 128), F32) for _, _, nc in PHASES],
            pltpu.VMEM((16, 128, 512), F32),
            pltpu.VMEM((2048, 512), BF16),
            pltpu.VMEM((2048, 512), BF16),
            pltpu.VMEM((16, 16, 16, 128), F32),
            pltpu.VMEM((256, 128), F32),
            pltpu.VMEM((3, 128, 128), F32),
            pltpu.VMEM((3, 64, 128), BF16),
            pltpu.VMEM((3, 64, 128), BF16),
            pltpu.VMEM((1024, 128), F32),
            pltpu.VMEM((1024, 128), F32),
            pltpu.VMEM((1024, 128), F32),
            pltpu.VMEM((512, 128), F32),
            pltpu.VMEM((3, 128, 128), F32),
            pltpu.VMEM((128, 128), F32),
            pltpu.VMEM((128, 128), F32),
            pltpu.VMEM((1, 16), F32),
            pltpu.VMEM((1, 128), F32),
            pltpu.VMEM((128, 128), F32),
            pltpu.SemaphoreType.DMA((9,)),
            pltpu.SemaphoreType.DMA((n_sem,)),
            pltpu.SemaphoreType.DMA((n_sem,)),
            pltpu.SemaphoreType.DMA((32,)),
            pltpu.SemaphoreType.DMA((32,)),
        ],
        compiler_params=pltpu.CompilerParams(
            collective_id=0, has_side_effects=True, vmem_limit_bytes=56 * 1024 * 1024
        ),
        cost_estimate=pl.CostEstimate(flops=2_000_000_000, bytes_accessed=8_000_000, transcendentals=0),
        name="ladder_cycle",
    )(amplitudes, ladder_ints, wts, occ_energy.reshape(1, -1), virt_energy.reshape(1, -1))
    return summed[None]


def solution(mesh):
    in_specs = (
        P("tensor", "contract", None),
        P("contract", None, "tensor"),
        P(None, None, None, "contract"),
        P(),
        P(),
    )
    out_specs = P(("tensor", "contract"), None, None)
    return jax.shard_map(body, mesh=mesh, in_specs=in_specs, out_specs=out_specs, check_vma=False)
```

```python
import jax
import jax.numpy as jnp
from jax import lax
from jax.experimental import pallas as pl
from jax.experimental.pallas import tpu as pltpu
from jax.sharding import PartitionSpec as P

F32 = jnp.float32
BF16 = jnp.bfloat16
NY, NZ, NX = 4, 8, 4
PH = 4
CP = 4
PHASES = (("yz", 0, 4), ("zy", 4, 7), ("zy", 11, 5))
ORDER = (
    "C0", "B0", "A0", "w", "B1", "B3", "C1", "A1", "B2", "A2", "B5", "C20",
    "C21", "B4", "B6", "A4", "v0", "v3", "C30", "A6", "C31", "v1", "B7", "B8",
    "B9", "C40", "A8", "A3", "v2", "A9", "C41", "A7", "A5", "Bt", "mB", "C5",
    "mC", "At", "mA",
)


def split(v):
    hi = v.astype(BF16)
    lo = (v - hi.astype(F32)).astype(BF16)
    return hi, lo


def dot3(a, b):
    ahi, alo = a
    bhi, blo = b
    out = jnp.dot(ahi, bhi, preferred_element_type=F32)
    out += jnp.dot(ahi, blo, preferred_element_type=F32)
    out += jnp.dot(alo, bhi, preferred_element_type=F32)
    return out


def kernel(
    amps, ints, wts, occ_in, virt_in, out,
    raw, gat_c, gat_a, gat_b, vraw, vhi, vlo, wraw, sel, selt, wl_hi, wl_lo, lad, cyc, part, got1, got2, fin, land, occ, virt, den,
    lsem, ssem, rsem, asend, arecv,
):
    gats = (gat_c, gat_a, gat_b)
    t = lax.axis_index("tensor")
    x = lax.axis_index("contract")
    h = t % 2
    u = t // 2
    z = u % NZ
    y = u // NZ

    def dev(yy, zz, hh, xx):
        return ((yy * NZ + zz) * 2 + hh, xx)

    sib = dev(y, z, 1 - h, x)

    def ymod(v):
        return (v + NY) % NY

    def zmod(v):
        return (v + NZ) % NZ

    bar = pltpu.get_barrier_semaphore()

    def greet(d):
        pl.semaphore_signal(bar, inc=1, device_id=d, device_id_type=pl.DeviceIdType.MESH)

    greet(sib)
    for dx in range(1, NX):
        greet((t, (x + dx) % NX))

    for dy in range(1, NY):
        greet(dev(ymod(y + dy), z, h, x))
    for dz in (1, 2, -1, -2):
        greet(dev(y, zmod(z + dz), h, x))

    wcopy = pltpu.make_async_copy(wts.at[:, :, pl.ds(h * 16, 16), :], wraw, lsem.at[0])
    acopy = pltpu.make_async_copy(
        amps.at[:, pl.ds(h * 16, 16), :], raw.at[pl.ds(h * 4, 4)], lsem.at[1]
    )
    acopy.start()
    own_cols = pl.multiple_of(h * 256, 256)
    sib_cols = pl.multiple_of((1 - h) * 256, 256)
    vcopies = [
        pltpu.make_async_copy(
            ints.at[pl.ds(h * 16 + q * CP, CP)],
            vraw.at[pl.ds(q * CP, CP), :, pl.ds(own_cols, 256)],
            lsem.at[2 + q],
        )
        for q in range(PH)
    ]
    wcopy.start()
    ecopies = [
        pltpu.make_async_copy(occ_in, occ, lsem.at[7]),
        pltpu.make_async_copy(virt_in, virt, lsem.at[8]),
    ]
    for c in ecopies:
        c.start()
    for c in vcopies:
        c.start()

    pl.semaphore_wait(bar, 1 + 3 + 3 + 4)

    sends = []

    def remote(n, src, dst, device):
        c = pltpu.make_async_remote_copy(
            src_ref=src, dst_ref=dst, send_sem=ssem.at[n], recv_sem=rsem.at[n],
            device_id=device, device_id_type=pl.DeviceIdType.MESH,
        )
        c.start()
        sends.append(c)

    def arrive(n, dst):
        pltpu.make_async_remote_copy(
            src_ref=dst, dst_ref=dst, send_sem=ssem.at[n], recv_sem=rsem.at[n],
            device_id=sib, device_id_type=pl.DeviceIdType.MESH,
        ).wait_recv()

    remote(0, amps.at[:, pl.ds((1 - h) * 16, 16), :], raw.at[pl.ds(h * 4, 4)], sib)
    for q in range(PH):
        remote(
            1 + q,
            ints.at[pl.ds((1 - h) * 16 + q * CP, CP)],
            vraw.at[pl.ds(q * CP, CP), :, pl.ds(own_cols, 256)],
            sib,
        )
    acopy.wait()
    arrive(0, raw.at[pl.ds((1 - h) * 4, 4)])

    for gat, (_, c0, nc) in zip(gats, PHASES):
        for c in range(nc):
            gat[y, z, c * 8:(c + 1) * 8, :] = raw[:, c0 + c, :]

    ids = {}

    def sem(key):
        return ids.setdefault(key, 8 + len(ids))

    def at_z(d):
        return (z + d + NZ) % NZ

    def at_y(d):
        return (y + d + NY) % NY

    def yz(q, k, pieces):
        gat = gats[q]

        def group(p, d):
            return gat.at[pl.ds(2 * p, 2), at_z(d)]

        def last(p, sign, step):
            return step < 4 or (p == 0) == (sign == 1)

        if k == 0:
            for dy in range(1, NY):
                remote(sem((q, "y", dy)), gat.at[y, z], gat.at[y, z], dev(at_y(dy), z, h, x))
            return
        if k == 1:
            for dy in range(1, NY):
                arrive(sem((q, "y", dy)), gat.at[at_y(-dy), z])
        for p in pieces:
            if k > 1:
                for sign in (1, -1):
                    if last(p, sign, k - 1):
                        arrive(sem((q, "z", k - 1, sign, p)), group(p, -sign * (k - 1)))
            if k < 5:
                for sign in (1, -1):
                    if last(p, sign, k):
                        b = group(p, -sign * (k - 1))
                        remote(sem((q, "z", k, sign, p)), b, b, dev(y, at_z(sign), h, x))

    def zy(q, k):
        gat = gats[q]
        rows = PHASES[q][2] * 8
        half = PHASES[q][2] // 2 * 8
        cut = {1: pl.ds(0, half), -1: pl.ds(half, rows - half)}

        def own_z(d):
            remote(sem((q, "z", d)), gat.at[y, z], gat.at[y, z], dev(y, at_z(d), h, x))

        def got_z(d):
            if abs(d) < 4:
                arrive(sem((q, "z", -d)), gat.at[y, at_z(d)])
            else:
                for sign in (1, -1):
                    arrive(sem((q, "z4", sign)), gat.at[y, at_z(4), cut[sign]])

        def forward_z(sign):
            b = gat.at[y, at_z(-2 * sign)]
            remote(sem((q, "z", 3 * sign)), b, b, dev(y, at_z(sign), h, x))
            c = gat.at[y, at_z(-2 * sign), cut[sign]]
            remote(sem((q, "z4", sign)), c, c, dev(y, at_z(2 * sign), h, x))

        def y1(d):
            for sign in (1, -1):
                b = gat.at[y, at_z(d)]
                remote(sem((q, "y1", d, sign)), b, b, dev(at_y(sign), z, h, x))

        def got_y1(d):
            for sign in (1, -1):
                arrive(sem((q, "y1", d, sign)), gat.at[at_y(-sign), at_z(d)])

        def y2(d, sign):
            b = gat.at[at_y(-sign), at_z(d)]
            remote(sem((q, "y2", d)), b, b, dev(at_y(sign), z, h, x))

        def got_y2(d):
            arrive(sem((q, "y2", d)), gat.at[at_y(2), at_z(d)])

        if k == 0:
            for d in (1, -1, 2, -2):
                own_z(d)
            y1(0)
        elif k == 1:
            got_z(1); got_z(-1)
            y1(1); y1(-1)
        elif k == 2:
            got_z(2); got_z(-2)
            forward_z(1); forward_z(-1)
            y1(2); y1(-2)
        elif k == 3:
            got_y1(0)
            y2(0, 1)
        elif k == 4:
            got_z(3); got_z(-3)
            y1(3); y1(-3)
        elif k == 5:
            got_y1(1); got_y1(-1)
            y2(1, 1); y2(-1, -1)
        elif k == 6:
            got_z(4)
            y1(4)
        elif k == 7:
            got_y1(2); got_y1(-2)
            y2(-2, 1); y2(2, -1)
        elif k == 8:
            got_y1(3); got_y1(-3)
            y2(3, 1); y2(-3, -1)
        elif k == 9:
            got_y1(4)
            y2(4, -1)
        elif k == 10:
            for d in (0, 1, -1, -2, 2, 3, -3, 4):
                got_y2(d)

    def prepare_ints(q):
        vcopies[q].wait()
        arrive(1 + q, vraw.at[pl.ds(q * CP, CP), :, pl.ds(sib_cols, 256)])

        def step(c, carry):
            cc = q * CP + c
            hi, lo = split(vraw[cc])
            at = pl.multiple_of(cc * 128, 128)
            vhi[pl.ds(at, 128), :] = hi
            vlo[pl.ds(at, 128), :] = lo
            return carry

        lax.fori_loop(0, CP, step, 0)

    def prepare_energies():
        for c in ecopies:
            c.wait()
        pair = t * NX + x
        who = lax.broadcasted_iota(jnp.int32, (1, 16), 1)
        o = occ[...]
        o = jnp.where(who == pair // 16, o, 0.0) + jnp.where(who == pair % 16, o, 0.0)
        v = jnp.broadcast_to(virt[...], (128, 128))
        den[...] = v.T + v - jnp.sum(o, axis=1, keepdims=True)

    def prepare_weights():
        wcopy.wait()
        lane = lax.broadcasted_iota(jnp.int32, (256, 128), 1)

        def step(i, acc):
            w = wraw[i].reshape(256, 128)
            shift = (4 * i - 4 * u + 128) % 128
            return jnp.where(lane // 4 == i, pltpu.roll(w, shift, 1), acc)

        sel[...] = lax.fori_loop(0, 16, step, jnp.zeros((256, 128), F32))
        for q, (_, c0, nc) in enumerate(PHASES):
            block = jnp.concatenate(
                [sel[pl.ds(c0 + c, 16, stride=16), :] for c in range(nc)], axis=0
            )
            block = jnp.concatenate([block, jnp.zeros((128 - nc * 16, 128), F32)], axis=0)
            selt[q] = block.T
            rows = jnp.concatenate(
                [selt.at[q][pl.ds(a, 16, stride=4), :] for a in range(4)], axis=0
            )
            hi, lo = split(rows)
            wl_hi[q] = hi
            wl_lo[q] = lo

    def ladder(q, first):
        gat = gats[q]
        _, c0, nc = PHASES[q]
        a = jnp.concatenate(
            [gat[:, :, c * 8:(c + 1) * 8, :].reshape(256, 128) for c in range(nc)], axis=1
        )
        ahi, alo = split(a)
        for n in range(2):
            cols = slice(n * 256, (n + 1) * 256)
            rows = slice(c0 * 128, (c0 + nc) * 128)
            r = dot3((ahi, alo), (vhi[rows, cols], vlo[rows, cols]))
            for m in range(2):
                at = slice((2 * n + m) * 256, (2 * n + m + 1) * 256)
                val = r[:, m * 128:(m + 1) * 128]
                if first:
                    lad[at, :] = val
                else:
                    lad[at, :] += val

    def cycle(q, first):
        _, c0, nc = PHASES[q]
        flat = gats[q].reshape(32 * nc * 8, 128)
        w = (wl_hi[q, :, 0:nc * 16], wl_lo[q, :, 0:nc * 16])

        def column(j):
            return jnp.concatenate(
                [
                    flat[pl.ds(((j // 8) * nc + c) * 8 + j % 8, 16, stride=2 * nc * 8), :]
                    for c in range(nc)
                ],
                axis=0,
            )

        for jp in range(8):
            b = jnp.concatenate([column(2 * jp), column(2 * jp + 1)], axis=1)
            r = dot3(w, split(b))
            for m in range(2):
                val = r[:, m * 128:(m + 1) * 128]
                at = slice((2 * jp + m) * 64, (2 * jp + m + 1) * 64)
                if first:
                    cyc[at, :] = val
                else:
                    cyc[at, :] += val

    first = True
    for step in ORDER:
        if step == "w":
            prepare_weights()
            prepare_energies()
        elif step[0] == "v":
            prepare_ints(int(step[1:]))
        elif step[0] == "m":
            q = "CAB".index(step[1])
            ladder(q, first)
            cycle(q, first)
            first = False
        else:
            q = "CAB".index(step[0])
            if PHASES[q][0] == "yz":
                yz(q, int(step[1]), [int(p) for p in step[2:]] or [0, 1])
            else:
                zy(q, 10 if step[1] == "t" else int(step[1:]))

    def assemble(s):
        for jh in range(2):
            for a in range(4):
                l = lad[pl.ds(a * 256 + 8 * jh + s, 16, stride=16), :]
                c = cyc[pl.ds((jh * 8 + s) * 64 + a * 16, 16), :]
                part[pl.ds((s * 32 + jh * 16) * 4 + a, 16, stride=4), :] = l + c

    for s in range(8):
        assemble(s)

    n_core = 5
    sib_rows = pl.multiple_of((1 - h) * 512, 512)
    own_rows = pl.multiple_of(h * 512, 512)
    remote(n_core, part.at[pl.ds(sib_rows, 512), :], got1, sib)
    arrive(n_core, got1)
    got1[...] = got1[...] + part[pl.ds(own_rows, 512), :]

    n_x = 8 + len(ids)
    for dx in (2, 1, 3):
        to = (x + dx) % NX
        remote(n_x + dx, got1.at[pl.ds(pl.multiple_of(to * 128, 128), 128), :], got2.at[dx - 1], (t, to))
    for dx in range(1, NX):
        arrive(n_x + dx, got2.at[dx - 1])
    mine = got1[pl.ds(pl.multiple_of(x * 128, 128), 128), :]
    fin[...] = mine + got2[0] + got2[1] + got2[2]

    def place(uu):
        return ((uu % 2) * 16 + uu // 2) * 4

    def a2a(k, to, frm):
        return pltpu.make_async_remote_copy(
            src_ref=fin.at[pl.ds(place(to), 4), :],
            dst_ref=land.at[pl.ds(frm * 4, 4), :],
            send_sem=asend.at[k], recv_sem=arecv.at[k],
            device_id=(to * 2 + h, x), device_id_type=pl.DeviceIdType.MESH,
        )

    def a2a_start(k, carry):
        a2a(k, (u + k) % 32, u).start()
        return carry

    lax.fori_loop(1, 32, a2a_start, 0)
    keep = pltpu.make_async_copy(fin.at[pl.ds(place(u), 4), :], land.at[pl.ds(u * 4, 4), :], lsem.at[6])
    keep.start()
    keep.wait()

    def a2a_wait(k, carry):
        a2a(k, (u + k) % 32, (u - k + 32) % 32).wait_recv()
        return carry

    lax.fori_loop(1, 32, a2a_wait, 0)
    out[...] = land[...] / den[...]

    def a2a_sent(k, carry):
        a2a(k, (u + k) % 32, u).wait_send()
        return carry

    lax.fori_loop(1, 32, a2a_sent, 0)
    for c in sends:
        c.wait_send()


def body(amplitudes, ladder_ints, cycle_ints, occ_energy, virt_energy):
    wts = jnp.transpose(cycle_ints, (0, 2, 3, 1))
    n_sem = 120
    summed = pl.pallas_call(
        kernel,
        out_shape=pltpu.VMEM((128, 128), F32),
        in_specs=[pl.BlockSpec(memory_space=pl.ANY)] * 5,
        out_specs=pl.BlockSpec(memory_space=pltpu.VMEM),
        scratch_shapes=[
            pltpu.VMEM((8, 16, 128), F32),
            *[pltpu.VMEM((NY, NZ, nc * 8, 128), F32) for _, _, nc in PHASES],
            pltpu.VMEM((16, 128, 512), F32),
            pltpu.VMEM((2048, 512), BF16),
            pltpu.VMEM((2048, 512), BF16),
            pltpu.VMEM((16, 16, 16, 128), F32),
            pltpu.VMEM((256, 128), F32),
            pltpu.VMEM((3, 128, 128), F32),
            pltpu.VMEM((3, 64, 128), BF16),
            pltpu.VMEM((3, 64, 128), BF16),
            pltpu.VMEM((1024, 128), F32),
            pltpu.VMEM((1024, 128), F32),
            pltpu.VMEM((1024, 128), F32),
            pltpu.VMEM((512, 128), F32),
            pltpu.VMEM((3, 128, 128), F32),
            pltpu.VMEM((128, 128), F32),
            pltpu.VMEM((128, 128), F32),
            pltpu.VMEM((1, 16), F32),
            pltpu.VMEM((1, 128), F32),
            pltpu.VMEM((128, 128), F32),
            pltpu.SemaphoreType.DMA((9,)),
            pltpu.SemaphoreType.DMA((n_sem,)),
            pltpu.SemaphoreType.DMA((n_sem,)),
            pltpu.SemaphoreType.DMA((32,)),
            pltpu.SemaphoreType.DMA((32,)),
        ],
        compiler_params=pltpu.CompilerParams(
            collective_id=0, has_side_effects=True, vmem_limit_bytes=56 * 1024 * 1024
        ),
        cost_estimate=pl.CostEstimate(flops=2_000_000_000, bytes_accessed=8_000_000, transcendentals=0),
        name="ladder_cycle",
    )(amplitudes, ladder_ints, wts, occ_energy.reshape(1, -1), virt_energy.reshape(1, -1))
    return summed[None]


def solution(mesh):
    in_specs = (
        P("tensor", "contract", None),
        P("contract", None, "tensor"),
        P(None, None, None, "contract"),
        P(),
        P(),
    )
    out_specs = P(("tensor", "contract"), None, None)
    return jax.shard_map(body, mesh=mesh, in_specs=in_specs, out_specs=out_specs, check_vma=False)
```

```python
import jax
import jax.numpy as jnp
from jax import lax
from jax.experimental import pallas as pl
from jax.experimental.pallas import tpu as pltpu
from jax.sharding import PartitionSpec as P

F32 = jnp.float32
BF16 = jnp.bfloat16
NY, NZ, NX = 4, 8, 4
PH = 4
CP = 4
PHASES = (("yz", 0, 4), ("zy", 4, 7), ("zy", 11, 5))
ORDER = (
    "C0", "B0", "A0", "w", "B1", "B3", "C1", "A1", "B2", "A2", "B5", "C20",
    "C21", "B4", "B6", "A4", "v0", "v3", "C30", "A6", "C31", "v1", "B7", "B8",
    "B9", "C40", "A8", "A3", "v2", "A9", "C41", "A7", "A5", "Bt", "mB", "C5",
    "mC", "At", "mA",
)


def split(v):
    hi = v.astype(BF16)
    lo = (v - hi.astype(F32)).astype(BF16)
    return hi, lo


def dot3(a, b):
    ahi, alo = a
    bhi, blo = b
    out = jnp.dot(ahi, bhi, preferred_element_type=F32)
    out += jnp.dot(ahi, blo, preferred_element_type=F32)
    out += jnp.dot(alo, bhi, preferred_element_type=F32)
    return out


def kernel(
    amps, ints, wts, occ_in, virt_in, out,
    raw, gat_c, gat_a, gat_b, vraw, vhi, vlo, wraw, sel, selt, wl_hi, wl_lo, lad, cyc, part, got1, got2, fin, land, occ, virt, den,
    lsem, ssem, rsem, asend, arecv,
):
    gats = (gat_c, gat_a, gat_b)
    t = lax.axis_index("tensor")
    x = lax.axis_index("contract")
    h = t % 2
    u = t // 2
    z = u % NZ
    y = u // NZ

    def dev(yy, zz, hh, xx):
        return ((yy * NZ + zz) * 2 + hh, xx)

    sib = dev(y, z, 1 - h, x)

    def ymod(v):
        return (v + NY) % NY

    def zmod(v):
        return (v + NZ) % NZ

    bar = pltpu.get_barrier_semaphore()

    def greet(d):
        pl.semaphore_signal(bar, inc=1, device_id=d, device_id_type=pl.DeviceIdType.MESH)

    greet(sib)
    for dx in range(1, NX):
        greet((t, (x + dx) % NX))

    for dy in range(1, NY):
        greet(dev(ymod(y + dy), z, h, x))
    for dz in (1, 2, -1, -2):
        greet(dev(y, zmod(z + dz), h, x))

    wcopy = pltpu.make_async_copy(wts.at[:, :, pl.ds(h * 16, 16), :], wraw, lsem.at[0])
    acopy = pltpu.make_async_copy(
        amps.at[:, pl.ds(h * 16, 16), :], raw.at[pl.ds(h * 4, 4)], lsem.at[1]
    )
    acopy.start()
    own_cols = pl.multiple_of(h * 256, 256)
    sib_cols = pl.multiple_of((1 - h) * 256, 256)
    vcopies = [
        pltpu.make_async_copy(
            ints.at[pl.ds(h * 16 + q * CP, CP)],
            vraw.at[pl.ds(q * CP, CP), :, pl.ds(own_cols, 256)],
            lsem.at[2 + q],
        )
        for q in range(PH)
    ]
    wcopy.start()
    ecopies = [
        pltpu.make_async_copy(occ_in, occ, lsem.at[7]),
        pltpu.make_async_copy(virt_in, virt, lsem.at[8]),
    ]
    for c in ecopies:
        c.start()
    for c in vcopies:
        c.start()

    pl.semaphore_wait(bar, 1 + 3 + 3 + 4)

    sends = []

    def remote(n, src, dst, device):
        c = pltpu.make_async_remote_copy(
            src_ref=src, dst_ref=dst, send_sem=ssem.at[n], recv_sem=rsem.at[n],
            device_id=device, device_id_type=pl.DeviceIdType.MESH,
        )
        c.start()
        sends.append(c)

    def arrive(n, dst):
        pltpu.make_async_remote_copy(
            src_ref=dst, dst_ref=dst, send_sem=ssem.at[n], recv_sem=rsem.at[n],
            device_id=sib, device_id_type=pl.DeviceIdType.MESH,
        ).wait_recv()

    remote(0, amps.at[:, pl.ds((1 - h) * 16, 16), :], raw.at[pl.ds(h * 4, 4)], sib)
    for q in range(PH):
        remote(
            1 + q,
            ints.at[pl.ds((1 - h) * 16 + q * CP, CP)],
            vraw.at[pl.ds(q * CP, CP), :, pl.ds(own_cols, 256)],
            sib,
        )
    acopy.wait()
    arrive(0, raw.at[pl.ds((1 - h) * 4, 4)])

    for gat, (_, c0, nc) in zip(gats, PHASES):
        for c in range(nc):
            gat[y, z, c * 8:(c + 1) * 8, :] = raw[:, c0 + c, :]

    ids = {}

    def sem(key):
        return ids.setdefault(key, 8 + len(ids))

    def at_z(d):
        return (z + d + NZ) % NZ

    def at_y(d):
        return (y + d + NY) % NY

    def yz(q, k, pieces):
        gat = gats[q]

        def group(p, d):
            return gat.at[pl.ds(2 * p, 2), at_z(d)]

        def last(p, sign, step):
            return step < 4 or (p == 0) == (sign == 1)

        if k == 0:
            for dy in range(1, NY):
                remote(sem((q, "y", dy)), gat.at[y, z], gat.at[y, z], dev(at_y(dy), z, h, x))
            return
        if k == 1:
            for dy in range(1, NY):
                arrive(sem((q, "y", dy)), gat.at[at_y(-dy), z])
        for p in pieces:
            if k > 1:
                for sign in (1, -1):
                    if last(p, sign, k - 1):
                        arrive(sem((q, "z", k - 1, sign, p)), group(p, -sign * (k - 1)))
            if k < 5:
                for sign in (1, -1):
                    if last(p, sign, k):
                        b = group(p, -sign * (k - 1))
                        remote(sem((q, "z", k, sign, p)), b, b, dev(y, at_z(sign), h, x))

    def zy(q, k):
        gat = gats[q]
        rows = PHASES[q][2] * 8
        half = PHASES[q][2] // 2 * 8
        cut = {1: pl.ds(0, half), -1: pl.ds(half, rows - half)}

        def own_z(d):
            remote(sem((q, "z", d)), gat.at[y, z], gat.at[y, z], dev(y, at_z(d), h, x))

        def got_z(d):
            if abs(d) < 4:
                arrive(sem((q, "z", -d)), gat.at[y, at_z(d)])
            else:
                for sign in (1, -1):
                    arrive(sem((q, "z4", sign)), gat.at[y, at_z(4), cut[sign]])

        def forward_z(sign):
            b = gat.at[y, at_z(-2 * sign)]
            remote(sem((q, "z", 3 * sign)), b, b, dev(y, at_z(sign), h, x))
            c = gat.at[y, at_z(-2 * sign), cut[sign]]
            remote(sem((q, "z4", sign)), c, c, dev(y, at_z(2 * sign), h, x))

        def y1(d):
            for sign in (1, -1):
                b = gat.at[y, at_z(d)]
                remote(sem((q, "y1", d, sign)), b, b, dev(at_y(sign), z, h, x))

        def got_y1(d):
            for sign in (1, -1):
                arrive(sem((q, "y1", d, sign)), gat.at[at_y(-sign), at_z(d)])

        def y2(d, sign):
            b = gat.at[at_y(-sign), at_z(d)]
            remote(sem((q, "y2", d)), b, b, dev(at_y(sign), z, h, x))

        def got_y2(d):
            arrive(sem((q, "y2", d)), gat.at[at_y(2), at_z(d)])

        if k == 0:
            for d in (1, -1, 2, -2):
                own_z(d)
            y1(0)
        elif k == 1:
            got_z(1); got_z(-1)
            y1(1); y1(-1)
        elif k == 2:
            got_z(2); got_z(-2)
            forward_z(1); forward_z(-1)
            y1(2); y1(-2)
        elif k == 3:
            got_y1(0)
            y2(0, 1)
        elif k == 4:
            got_z(3); got_z(-3)
            y1(3); y1(-3)
        elif k == 5:
            got_y1(1); got_y1(-1)
            y2(1, 1); y2(-1, -1)
        elif k == 6:
            got_z(4)
            y1(4)
        elif k == 7:
            got_y1(2); got_y1(-2)
            y2(-2, 1); y2(2, -1)
        elif k == 8:
            got_y1(3); got_y1(-3)
            y2(3, 1); y2(-3, -1)
        elif k == 9:
            got_y1(4)
            y2(4, -1)
        elif k == 10:
            for d in (0, 1, -1, -2, 2, 3, -3, 4):
                got_y2(d)

    def prepare_ints(q):
        vcopies[q].wait()
        arrive(1 + q, vraw.at[pl.ds(q * CP, CP), :, pl.ds(sib_cols, 256)])

        def step(c, carry):
            cc = q * CP + c
            hi, lo = split(vraw[cc])
            at = pl.multiple_of(cc * 128, 128)
            vhi[pl.ds(at, 128), :] = hi
            vlo[pl.ds(at, 128), :] = lo
            return carry

        lax.fori_loop(0, CP, step, 0)

    def prepare_energies():
        for c in ecopies:
            c.wait()
        pair = t * NX + x
        who = lax.broadcasted_iota(jnp.int32, (1, 16), 1)
        o = occ[...]
        o = jnp.where(who == pair // 16, o, 0.0) + jnp.where(who == pair % 16, o, 0.0)
        v = jnp.broadcast_to(virt[...], (128, 128))
        den[...] = v.T + v - jnp.sum(o, axis=1, keepdims=True)

    def prepare_weights():
        wcopy.wait()
        lane = lax.broadcasted_iota(jnp.int32, (256, 128), 1)

        def step(i, acc):
            w = wraw[i].reshape(256, 128)
            shift = (4 * i - 4 * u + 128) % 128
            return jnp.where(lane // 4 == i, pltpu.roll(w, shift, 1), acc)

        sel[...] = lax.fori_loop(0, 16, step, jnp.zeros((256, 128), F32))
        for q, (_, c0, nc) in enumerate(PHASES):
            block = jnp.concatenate(
                [sel[pl.ds(c0 + c, 16, stride=16), :] for c in range(nc)], axis=0
            )
            block = jnp.concatenate([block, jnp.zeros((128 - nc * 16, 128), F32)], axis=0)
            selt[q] = block.T
            rows = jnp.concatenate(
                [selt.at[q][pl.ds(a, 16, stride=4), :] for a in range(4)], axis=0
            )
            hi, lo = split(rows)
            wl_hi[q] = hi
            wl_lo[q] = lo

    def ladder(q, first):
        gat = gats[q]
        _, c0, nc = PHASES[q]
        a = jnp.concatenate(
            [gat[:, :, c * 8:(c + 1) * 8, :].reshape(256, 128) for c in range(nc)], axis=1
        )
        ahi, alo = split(a)
        for n in range(2):
            cols = slice(n * 256, (n + 1) * 256)
            rows = slice(c0 * 128, (c0 + nc) * 128)
            r = dot3((ahi, alo), (vhi[rows, cols], vlo[rows, cols]))
            for m in range(2):
                at = slice((2 * n + m) * 256, (2 * n + m + 1) * 256)
                val = r[:, m * 128:(m + 1) * 128]
                if first:
                    lad[at, :] = val
                else:
                    lad[at, :] += val

    def cycle(q, first):
        _, c0, nc = PHASES[q]
        flat = gats[q].reshape(32 * nc * 8, 128)
        w = (wl_hi[q, :, 0:nc * 16], wl_lo[q, :, 0:nc * 16])

        def column(j):
            return jnp.concatenate(
                [
                    flat[pl.ds(((j // 8) * nc + c) * 8 + j % 8, 16, stride=2 * nc * 8), :]
                    for c in range(nc)
                ],
                axis=0,
            )

        for jp in range(8):
            b = jnp.concatenate([column(2 * jp), column(2 * jp + 1)], axis=1)
            r = dot3(w, split(b))
            for m in range(2):
                val = r[:, m * 128:(m + 1) * 128]
                at = slice((2 * jp + m) * 64, (2 * jp + m + 1) * 64)
                if first:
                    cyc[at, :] = val
                else:
                    cyc[at, :] += val

    first = True
    for step in ORDER:
        if step == "w":
            prepare_weights()
            prepare_energies()
        elif step[0] == "v":
            prepare_ints(int(step[1:]))
        elif step[0] == "m":
            q = "CAB".index(step[1])
            ladder(q, first)
            cycle(q, first)
            first = False
        else:
            q = "CAB".index(step[0])
            if PHASES[q][0] == "yz":
                yz(q, int(step[1]), [int(p) for p in step[2:]] or [0, 1])
            else:
                zy(q, 10 if step[1] == "t" else int(step[1:]))

    def assemble(s):
        for jh in range(2):
            for a in range(4):
                l = lad[pl.ds(a * 256 + 8 * jh + s, 16, stride=16), :]
                c = cyc[pl.ds((jh * 8 + s) * 64 + a * 16, 16), :]
                part[pl.ds((s * 32 + jh * 16) * 4 + a, 16, stride=4), :] = l + c

    for s in range(8):
        assemble(s)

    n_core = 5
    sib_rows = pl.multiple_of((1 - h) * 512, 512)
    own_rows = pl.multiple_of(h * 512, 512)
    remote(n_core, part.at[pl.ds(sib_rows, 512), :], got1, sib)
    arrive(n_core, got1)
    got1[...] = got1[...] + part[pl.ds(own_rows, 512), :]

    n_x = 8 + len(ids)
    for dx in (2, 1, 3):
        to = (x + dx) % NX
        remote(n_x + dx, got1.at[pl.ds(pl.multiple_of(to * 128, 128), 128), :], got2.at[dx - 1], (t, to))
    for dx in range(1, NX):
        arrive(n_x + dx, got2.at[dx - 1])
    mine = got1[pl.ds(pl.multiple_of(x * 128, 128), 128), :]
    fin[...] = mine + got2[0] + got2[1] + got2[2]

    def place(uu):
        return ((uu % 2) * 16 + uu // 2) * 4

    def a2a(k, to, frm):
        return pltpu.make_async_remote_copy(
            src_ref=fin.at[pl.ds(place(to), 4), :],
            dst_ref=land.at[pl.ds(frm * 4, 4), :],
            send_sem=asend.at[0], recv_sem=arecv.at[0],
            device_id=(to * 2 + h, x), device_id_type=pl.DeviceIdType.MESH,
        )

    def a2a_start(k, carry):
        a2a(k, (u + k) % 32, u).start()
        return carry

    lax.fori_loop(1, 32, a2a_start, 0)
    keep = pltpu.make_async_copy(fin.at[pl.ds(place(u), 4), :], land.at[pl.ds(u * 4, 4), :], lsem.at[6])
    keep.start()
    keep.wait()

    for c in sends:
        c.wait_send()

    rest = pltpu.make_async_remote_copy(
        src_ref=fin.at[pl.ds(0, 124), :],
        dst_ref=land.at[pl.ds(0, 124), :],
        send_sem=asend.at[0], recv_sem=arecv.at[0],
        device_id=sib, device_id_type=pl.DeviceIdType.MESH,
    )
    rest.wait_recv()
    out[...] = land[...] / den[...]

    rest.wait_send()


def body(amplitudes, ladder_ints, cycle_ints, occ_energy, virt_energy):
    wts = jnp.transpose(cycle_ints, (0, 2, 3, 1))
    n_sem = 120
    summed = pl.pallas_call(
        kernel,
        out_shape=pltpu.VMEM((128, 128), F32),
        in_specs=[pl.BlockSpec(memory_space=pl.ANY)] * 5,
        out_specs=pl.BlockSpec(memory_space=pltpu.VMEM),
        scratch_shapes=[
            pltpu.VMEM((8, 16, 128), F32),
            *[pltpu.VMEM((NY, NZ, nc * 8, 128), F32) for _, _, nc in PHASES],
            pltpu.VMEM((16, 128, 512), F32),
            pltpu.VMEM((2048, 512), BF16),
            pltpu.VMEM((2048, 512), BF16),
            pltpu.VMEM((16, 16, 16, 128), F32),
            pltpu.VMEM((256, 128), F32),
            pltpu.VMEM((3, 128, 128), F32),
            pltpu.VMEM((3, 64, 128), BF16),
            pltpu.VMEM((3, 64, 128), BF16),
            pltpu.VMEM((1024, 128), F32),
            pltpu.VMEM((1024, 128), F32),
            pltpu.VMEM((1024, 128), F32),
            pltpu.VMEM((512, 128), F32),
            pltpu.VMEM((3, 128, 128), F32),
            pltpu.VMEM((128, 128), F32),
            pltpu.VMEM((128, 128), F32),
            pltpu.VMEM((1, 16), F32),
            pltpu.VMEM((1, 128), F32),
            pltpu.VMEM((128, 128), F32),
            pltpu.SemaphoreType.DMA((9,)),
            pltpu.SemaphoreType.DMA((n_sem,)),
            pltpu.SemaphoreType.DMA((n_sem,)),
            pltpu.SemaphoreType.DMA((1,)),
            pltpu.SemaphoreType.DMA((1,)),
        ],
        compiler_params=pltpu.CompilerParams(
            collective_id=0, has_side_effects=True, vmem_limit_bytes=56 * 1024 * 1024
        ),
        cost_estimate=pl.CostEstimate(flops=2_000_000_000, bytes_accessed=8_000_000, transcendentals=0),
        name="ladder_cycle",
    )(amplitudes, ladder_ints, wts, occ_energy.reshape(1, -1), virt_energy.reshape(1, -1))
    return summed[None]


def solution(mesh):
    in_specs = (
        P("tensor", "contract", None),
        P("contract", None, "tensor"),
        P(None, None, None, "contract"),
        P(),
        P(),
    )
    out_specs = P(("tensor", "contract"), None, None)
    return jax.shard_map(body, mesh=mesh, in_specs=in_specs, out_specs=out_specs, check_vma=False)
```

```python
import jax
import jax.numpy as jnp
from jax import lax
from jax.experimental import pallas as pl
from jax.experimental.pallas import tpu as pltpu
from jax.sharding import PartitionSpec as P

F32 = jnp.float32
BF16 = jnp.bfloat16
NY, NZ, NX = 4, 8, 4
PH = 4
CP = 4
PHASES = (("yz", 0, 4), ("zy", 4, 7), ("zy", 11, 5))
ORDER = (
    "C0", "B0", "A0", "w", "B1", "B3", "C1", "A1", "B2", "A2", "B5", "C20",
    "C21", "B4", "B6", "A4", "v0", "v3", "C30", "A6", "C31", "v1", "B7", "B8",
    "B9", "C40", "A8", "A3", "v2", "A9", "C41", "A7", "A5", "Bt", "mB", "C5",
    "mC", "At", "mA",
)


def split(v):
    hi = v.astype(BF16)
    lo = (v - hi.astype(F32)).astype(BF16)
    return hi, lo


def dot3(a, b):
    ahi, alo = a
    bhi, blo = b
    out = jnp.dot(ahi, bhi, preferred_element_type=F32)
    out += jnp.dot(ahi, blo, preferred_element_type=F32)
    out += jnp.dot(alo, bhi, preferred_element_type=F32)
    return out


def kernel(
    amps, ints, wts, occ_in, virt_in, out,
    raw, gat_c, gat_a, gat_b, vraw, vhi, vlo, wraw, sel, selt, wl_hi, wl_lo, lad, cyc, part, got1, got2, fin, land, occ, virt, den,
    lsem, ssem, rsem, asend, arecv,
):
    gats = (gat_c, gat_a, gat_b)
    t = lax.axis_index("tensor")
    x = lax.axis_index("contract")
    h = t % 2
    u = t // 2
    z = u % NZ
    y = u // NZ

    def dev(yy, zz, hh, xx):
        return ((yy * NZ + zz) * 2 + hh, xx)

    sib = dev(y, z, 1 - h, x)

    def ymod(v):
        return (v + NY) % NY

    def zmod(v):
        return (v + NZ) % NZ

    bar = pltpu.get_barrier_semaphore()

    def greet(d):
        pl.semaphore_signal(bar, inc=1, device_id=d, device_id_type=pl.DeviceIdType.MESH)

    greet(sib)
    for dx in range(1, NX):
        greet((t, (x + dx) % NX))

    for dy in range(1, NY):
        greet(dev(ymod(y + dy), z, h, x))
    for dz in (1, 2, -1, -2):
        greet(dev(y, zmod(z + dz), h, x))

    wcopy = pltpu.make_async_copy(wts.at[:, :, pl.ds(h * 16, 16), :], wraw, lsem.at[0])
    acopy = pltpu.make_async_copy(
        amps.at[:, pl.ds(h * 16, 16), :], raw.at[pl.ds(h * 4, 4)], lsem.at[1]
    )
    acopy.start()
    own_cols = pl.multiple_of(h * 256, 256)
    sib_cols = pl.multiple_of((1 - h) * 256, 256)
    vcopies = [
        pltpu.make_async_copy(
            ints.at[pl.ds(h * 16 + q * CP, CP)],
            vraw.at[pl.ds(q * CP, CP), :, pl.ds(own_cols, 256)],
            lsem.at[2 + q],
        )
        for q in range(PH)
    ]
    wcopy.start()
    ecopies = [
        pltpu.make_async_copy(occ_in, occ, lsem.at[7]),
        pltpu.make_async_copy(virt_in, virt, lsem.at[8]),
    ]
    for c in ecopies:
        c.start()
    for c in vcopies:
        c.start()

    pl.semaphore_wait(bar, 1 + 3 + 3 + 4)

    sends = []

    def remote(n, src, dst, device):
        c = pltpu.make_async_remote_copy(
            src_ref=src, dst_ref=dst, send_sem=ssem.at[len(sends)], recv_sem=rsem.at[n],
            device_id=device, device_id_type=pl.DeviceIdType.MESH,
        )
        c.start()
        sends.append(c)

    def arrive(n, dst):
        pltpu.make_async_remote_copy(
            src_ref=dst, dst_ref=dst, send_sem=ssem.at[0], recv_sem=rsem.at[n],
            device_id=sib, device_id_type=pl.DeviceIdType.MESH,
        ).wait_recv()

    remote(0, amps.at[:, pl.ds((1 - h) * 16, 16), :], raw.at[pl.ds(h * 4, 4)], sib)
    for q in range(PH):
        remote(
            1 + q,
            ints.at[pl.ds((1 - h) * 16 + q * CP, CP)],
            vraw.at[pl.ds(q * CP, CP), :, pl.ds(own_cols, 256)],
            sib,
        )
    acopy.wait()
    arrive(0, raw.at[pl.ds((1 - h) * 4, 4)])

    for gat, (_, c0, nc) in zip(gats, PHASES):
        for c in range(nc):
            gat[y, z, c * 8:(c + 1) * 8, :] = raw[:, c0 + c, :]

    ids = {}

    def sem(key):
        return ids.setdefault(key, 8 + len(ids))

    def at_z(d):
        return (z + d + NZ) % NZ

    def at_y(d):
        return (y + d + NY) % NY

    def yz(q, k, pieces):
        gat = gats[q]

        def group(p, d):
            return gat.at[pl.ds(2 * p, 2), at_z(d)]

        def last(p, sign, step):
            return step < 4 or (p == 0) == (sign == 1)

        if k == 0:
            for dy in range(1, NY):
                remote(sem((q, "y")), gat.at[y, z], gat.at[y, z], dev(at_y(dy), z, h, x))
            return
        if k == 1:
            arrive(sem((q, "y")), gat.at[0:3, z])
        for p in pieces:
            if k > 1:
                both = gat.at[:, z] if k < 5 else group(p, 4)
                arrive(sem((q, "z", k - 1, p)), both)
            if k < 5:
                for sign in (1, -1):
                    if last(p, sign, k):
                        b = group(p, -sign * (k - 1))
                        remote(sem((q, "z", k, p)), b, b, dev(y, at_z(sign), h, x))

    def zy(q, k):
        gat = gats[q]
        rows = PHASES[q][2] * 8
        half = PHASES[q][2] // 2 * 8
        cut = {1: pl.ds(0, half), -1: pl.ds(half, rows - half)}

        def own_z(d):
            remote(sem((q, "z", abs(d))), gat.at[y, z], gat.at[y, z], dev(y, at_z(d), h, x))

        def got_z(d):
            arrive(sem((q, "z", d)), gat.at[0:2, z] if d < 4 else gat.at[y, at_z(4)])

        def forward_z(sign):
            b = gat.at[y, at_z(-2 * sign)]
            remote(sem((q, "z", 3)), b, b, dev(y, at_z(sign), h, x))
            c = gat.at[y, at_z(-2 * sign), cut[sign]]
            remote(sem((q, "z", 4)), c, c, dev(y, at_z(2 * sign), h, x))

        def y1(d):
            for sign in (1, -1):
                b = gat.at[y, at_z(d)]
                remote(sem((q, "y1", d)), b, b, dev(at_y(sign), z, h, x))

        def got_y1(d):
            arrive(sem((q, "y1", d)), gat.at[0:2, z])

        def y2(d, sign):
            b = gat.at[at_y(-sign), at_z(d)]
            remote(sem((q, "y2")), b, b, dev(at_y(sign), z, h, x))

        if k == 0:
            for d in (1, -1, 2, -2):
                own_z(d)
            y1(0)
        elif k == 1:
            got_z(1)
            y1(1); y1(-1)
        elif k == 2:
            got_z(2)
            forward_z(1); forward_z(-1)
            y1(2); y1(-2)
        elif k == 3:
            got_y1(0)
            y2(0, 1)
        elif k == 4:
            got_z(3)
            y1(3); y1(-3)
        elif k == 5:
            got_y1(1); got_y1(-1)
            y2(1, 1); y2(-1, -1)
        elif k == 6:
            got_z(4)
            y1(4)
        elif k == 7:
            got_y1(2); got_y1(-2)
            y2(-2, 1); y2(2, -1)
        elif k == 8:
            got_y1(3); got_y1(-3)
            y2(3, 1); y2(-3, -1)
        elif k == 9:
            got_y1(4)
            y2(4, -1)
        elif k == 10:
            arrive(sem((q, "y2")), gat.at[at_y(2)])

    def prepare_ints(q):
        vcopies[q].wait()
        arrive(1 + q, vraw.at[pl.ds(q * CP, CP), :, pl.ds(sib_cols, 256)])

        def step(c, carry):
            cc = q * CP + c
            hi, lo = split(vraw[cc])
            at = pl.multiple_of(cc * 128, 128)
            vhi[pl.ds(at, 128), :] = hi
            vlo[pl.ds(at, 128), :] = lo
            return carry

        lax.fori_loop(0, CP, step, 0)

    def prepare_energies():
        for c in ecopies:
            c.wait()
        pair = t * NX + x
        who = lax.broadcasted_iota(jnp.int32, (1, 16), 1)
        o = occ[...]
        o = jnp.where(who == pair // 16, o, 0.0) + jnp.where(who == pair % 16, o, 0.0)
        v = jnp.broadcast_to(virt[...], (128, 128))
        den[...] = v.T + v - jnp.sum(o, axis=1, keepdims=True)

    def prepare_weights():
        wcopy.wait()
        lane = lax.broadcasted_iota(jnp.int32, (256, 128), 1)

        def step(i, acc):
            w = wraw[i].reshape(256, 128)
            shift = (4 * i - 4 * u + 128) % 128
            return jnp.where(lane // 4 == i, pltpu.roll(w, shift, 1), acc)

        sel[...] = lax.fori_loop(0, 16, step, jnp.zeros((256, 128), F32))
        for q, (_, c0, nc) in enumerate(PHASES):
            block = jnp.concatenate(
                [sel[pl.ds(c0 + c, 16, stride=16), :] for c in range(nc)], axis=0
            )
            block = jnp.concatenate([block, jnp.zeros((128 - nc * 16, 128), F32)], axis=0)
            selt[q] = block.T
            rows = jnp.concatenate(
                [selt.at[q][pl.ds(a, 16, stride=4), :] for a in range(4)], axis=0
            )
            hi, lo = split(rows)
            wl_hi[q] = hi
            wl_lo[q] = lo

    def ladder(q, first):
        gat = gats[q]
        _, c0, nc = PHASES[q]
        a = jnp.concatenate(
            [gat[:, :, c * 8:(c + 1) * 8, :].reshape(256, 128) for c in range(nc)], axis=1
        )
        ahi, alo = split(a)
        for n in range(2):
            cols = slice(n * 256, (n + 1) * 256)
            rows = slice(c0 * 128, (c0 + nc) * 128)
            r = dot3((ahi, alo), (vhi[rows, cols], vlo[rows, cols]))
            for m in range(2):
                at = slice((2 * n + m) * 256, (2 * n + m + 1) * 256)
                val = r[:, m * 128:(m + 1) * 128]
                if first:
                    lad[at, :] = val
                else:
                    lad[at, :] += val

    def cycle(q, first):
        _, c0, nc = PHASES[q]
        flat = gats[q].reshape(32 * nc * 8, 128)
        w = (wl_hi[q, :, 0:nc * 16], wl_lo[q, :, 0:nc * 16])

        def column(j):
            return jnp.concatenate(
                [
                    flat[pl.ds(((j // 8) * nc + c) * 8 + j % 8, 16, stride=2 * nc * 8), :]
                    for c in range(nc)
                ],
                axis=0,
            )

        for jp in range(8):
            b = jnp.concatenate([column(2 * jp), column(2 * jp + 1)], axis=1)
            r = dot3(w, split(b))
            for m in range(2):
                val = r[:, m * 128:(m + 1) * 128]
                at = slice((2 * jp + m) * 64, (2 * jp + m + 1) * 64)
                if first:
                    cyc[at, :] = val
                else:
                    cyc[at, :] += val

    first = True
    for step in ORDER:
        if step == "w":
            prepare_weights()
            prepare_energies()
        elif step[0] == "v":
            prepare_ints(int(step[1:]))
        elif step[0] == "m":
            q = "CAB".index(step[1])
            ladder(q, first)
            cycle(q, first)
            first = False
        else:
            q = "CAB".index(step[0])
            if PHASES[q][0] == "yz":
                yz(q, int(step[1]), [int(p) for p in step[2:]] or [0, 1])
            else:
                zy(q, 10 if step[1] == "t" else int(step[1:]))

    def assemble(s):
        for jh in range(2):
            for a in range(4):
                l = lad[pl.ds(a * 256 + 8 * jh + s, 16, stride=16), :]
                c = cyc[pl.ds((jh * 8 + s) * 64 + a * 16, 16), :]
                part[pl.ds((s * 32 + jh * 16) * 4 + a, 16, stride=4), :] = l + c

    for s in range(8):
        assemble(s)

    n_core = 5
    sib_rows = pl.multiple_of((1 - h) * 512, 512)
    own_rows = pl.multiple_of(h * 512, 512)
    remote(n_core, part.at[pl.ds(sib_rows, 512), :], got1, sib)
    arrive(n_core, got1)
    got1[...] = got1[...] + part[pl.ds(own_rows, 512), :]

    n_x = 8 + len(ids)
    for dx in (2, 1, 3):
        to = (x + dx) % NX
        remote(n_x + dx, got1.at[pl.ds(pl.multiple_of(to * 128, 128), 128), :], got2.at[dx - 1], (t, to))
    for dx in range(1, NX):
        arrive(n_x + dx, got2.at[dx - 1])
    mine = got1[pl.ds(pl.multiple_of(x * 128, 128), 128), :]
    fin[...] = mine + got2[0] + got2[1] + got2[2]

    def place(uu):
        return ((uu % 2) * 16 + uu // 2) * 4

    def a2a(k, to, frm):
        return pltpu.make_async_remote_copy(
            src_ref=fin.at[pl.ds(place(to), 4), :],
            dst_ref=land.at[pl.ds(frm * 4, 4), :],
            send_sem=asend.at[0], recv_sem=arecv.at[0],
            device_id=(to * 2 + h, x), device_id_type=pl.DeviceIdType.MESH,
        )

    def a2a_start(k, carry):
        a2a(k, (u + k) % 32, u).start()
        return carry

    for k in range(1, 32):
        a2a_start(k, 0)
    keep = pltpu.make_async_copy(fin.at[pl.ds(place(u), 4), :], land.at[pl.ds(u * 4, 4), :], lsem.at[6])
    keep.start()
    keep.wait()

    for c in sends:
        c.wait_send()

    rest = pltpu.make_async_remote_copy(
        src_ref=fin.at[pl.ds(0, 124), :],
        dst_ref=land.at[pl.ds(0, 124), :],
        send_sem=asend.at[0], recv_sem=arecv.at[0],
        device_id=sib, device_id_type=pl.DeviceIdType.MESH,
    )
    rest.wait_recv()
    out[...] = land[...] / den[...]

    rest.wait_send()


def body(amplitudes, ladder_ints, cycle_ints, occ_energy, virt_energy):
    wts = jnp.transpose(cycle_ints, (0, 2, 3, 1))
    n_sem = 120
    summed = pl.pallas_call(
        kernel,
        out_shape=pltpu.VMEM((128, 128), F32),
        in_specs=[pl.BlockSpec(memory_space=pl.ANY)] * 5,
        out_specs=pl.BlockSpec(memory_space=pltpu.VMEM),
        scratch_shapes=[
            pltpu.VMEM((8, 16, 128), F32),
            *[pltpu.VMEM((NY, NZ, nc * 8, 128), F32) for _, _, nc in PHASES],
            pltpu.VMEM((16, 128, 512), F32),
            pltpu.VMEM((2048, 512), BF16),
            pltpu.VMEM((2048, 512), BF16),
            pltpu.VMEM((16, 16, 16, 128), F32),
            pltpu.VMEM((256, 128), F32),
            pltpu.VMEM((3, 128, 128), F32),
            pltpu.VMEM((3, 64, 128), BF16),
            pltpu.VMEM((3, 64, 128), BF16),
            pltpu.VMEM((1024, 128), F32),
            pltpu.VMEM((1024, 128), F32),
            pltpu.VMEM((1024, 128), F32),
            pltpu.VMEM((512, 128), F32),
            pltpu.VMEM((3, 128, 128), F32),
            pltpu.VMEM((128, 128), F32),
            pltpu.VMEM((128, 128), F32),
            pltpu.VMEM((1, 16), F32),
            pltpu.VMEM((1, 128), F32),
            pltpu.VMEM((128, 128), F32),
            pltpu.SemaphoreType.DMA((9,)),
            pltpu.SemaphoreType.DMA((n_sem,)),
            pltpu.SemaphoreType.DMA((n_sem,)),
            pltpu.SemaphoreType.DMA((1,)),
            pltpu.SemaphoreType.DMA((1,)),
        ],
        compiler_params=pltpu.CompilerParams(
            collective_id=0, has_side_effects=True, vmem_limit_bytes=56 * 1024 * 1024
        ),
        cost_estimate=pl.CostEstimate(flops=2_000_000_000, bytes_accessed=8_000_000, transcendentals=0),
        name="ladder_cycle",
    )(amplitudes, ladder_ints, wts, occ_energy.reshape(1, -1), virt_energy.reshape(1, -1))
    return summed[None]


def solution(mesh):
    in_specs = (
        P("tensor", "contract", None),
        P("contract", None, "tensor"),
        P(None, None, None, "contract"),
        P(),
        P(),
    )
    out_specs = P(("tensor", "contract"), None, None)
    return jax.shard_map(body, mesh=mesh, in_specs=in_specs, out_specs=out_specs, check_vma=False)
```
